128 devices in a mesh: grp: 32 (over x, y, z_hi), tp: 4 (over z_lo, core).
Axes of the slice: x: 4, y: 4, z: 4 (z_hi: 2, z_lo: 2; z = z_hi * 2 + z_lo), core: 2. Of those that a mesh axis runs over, the one named last changes fastest.
Arguments:
- queries: bfloat16 [256, 4, 128, 192], P('grp', None, 'tp'), may hold values from -500 to 500
- new_kv: bfloat16 [256, 4, 576], P('grp'), may hold values from -8 to 8
- owner_index: int32 [1], replicated, may hold values from 0 to 31
- prefix_latent: bfloat16 [32, 8192, 512], P('grp'), may hold values from -6 to 6
- prefix_rope: bfloat16 [32, 64, 8192], P('grp'), may hold values from -6 to 6
- key_up: bfloat16 [128, 128, 512], P('tp'), may hold values from -0.25 to 0.25
- value_up: bfloat16 [128, 512, 128], P('tp'), may hold values from -0.25 to 0.25
- out_weight: bfloat16 [16384, 7168], P('tp', 'grp'), may hold values from -2.5 to 2.5
Outputs:
- layer_out: bfloat16 [256, 4, 7168], P('tp', None, 'grp')
The draws below stay inside these ranges and needn't reach their ends.
All inputs are finite; a program needn't handle non-finite values.
Results may differ from the reference program's by a relative error of at most 0.015.
Values may be sent and summed in bfloat16 or wider, within the bound.
A program may use at most 192 MiB of HBM per device.

```python
import jax
import jax.numpy as jnp
from jax import lax

D = 7168
HEADS = 128
LAT = 512
ROPE = 64
NOPE = 128
VDIM = 128
PREFIX = 8192
STEPS = 4
SAMPLES = 256
N_GRP = 32


def common_rope(key):
    jitter = jax.random.normal(jax.random.fold_in(key, 102), (SAMPLES, STEPS, ROPE), jnp.float32)
    return jitter


def draw_new_kv(key, part):
    jitter = common_rope(key)
    key = jax.random.fold_in(key, 1)
    latent_part = jax.random.normal(key, (SAMPLES, STEPS, LAT), jnp.float32)
    rope_part = jitter
    joined = jnp.concatenate([latent_part, rope_part], axis=2)
    return jnp.clip(joined, -6.0, 6.0).astype(jnp.bfloat16)


def draw_queries(key, part):
    key = jax.random.fold_in(key, 2)
    drawn = jax.random.normal(key, (SAMPLES, STEPS, HEADS, NOPE + ROPE), jnp.float32)
    drawn = jnp.clip(drawn, -6.0, 6.0)
    return drawn.astype(jnp.bfloat16)


def levels(key, dims, shards, low, largest):
    def one(position, blocks):
        draws = jax.random.uniform(jax.random.fold_in(jax.random.fold_in(key, 6), position), (blocks,), jnp.float32, low / len(shards), largest / len(shards))
        return jnp.repeat(jnp.exp(draws), dims[position] // blocks).reshape((-1,) + (1,) * (len(dims) - position - 1))

    level = one(*shards[0])
    for cut in shards[1:]:
        level = level * one(*cut)
    return level


def centred(rng, shape, width, limit, cuts=(), kind=jnp.bfloat16):
    result = width * jax.random.normal(rng, shape, jnp.float32)
    if cuts:
        result = result * levels(rng, shape, cuts, -0.22, 0.18)
    return jnp.clip(result, -limit, limit).astype(kind)


def setup_inputs(seed: int = 0) -> dict:
    splits = jax.random.split(jax.random.key(seed), 9)
    queries = draw_queries(jax.random.fold_in(splits[8], 71), 0)
    new_kv = draw_new_kv(jax.random.fold_in(splits[8], 71), 0)
    owner_index = jax.random.randint(splits[2], (1,), 0, N_GRP).astype(jnp.int32)
    prefix_latent = centred(splits[3], (N_GRP, PREFIX, LAT), 1.0, 6.0, ((0, 32),))
    prefix_rope = centred(splits[4], (N_GRP, ROPE, PREFIX), 1.0, 6.0, ((0, 32),))
    key_up = centred(splits[5], (HEADS, NOPE, LAT), LAT ** -0.5, 0.25, ((0, 4),))
    value_up = centred(splits[6], (HEADS, LAT, VDIM), LAT ** -0.5, 0.25, ((0, 4),))
    out_weight = centred(splits[7], (HEADS * VDIM, D), (max(1, HEADS * VDIM * 3 // PREFIX)) ** -0.5, 2.5, ((0, 4), (1, 32)))
    return dict(queries=queries, new_kv=new_kv, owner_index=owner_index, prefix_latent=prefix_latent, prefix_rope=prefix_rope, key_up=key_up, value_up=value_up, out_weight=out_weight)


def attend_sample(sample_query, sample_new, latent, rotary, key_up, value_up):
    query_width = sample_query.shape[-1]
    nope_width = key_up.shape[1]
    latent_width = key_up.shape[2]
    score_scale = query_width ** -0.5
    q_nope = sample_query[:, :, :nope_width].astype(jnp.float32)
    q_rope = sample_query[:, :, nope_width:].astype(jnp.float32)
    q_latent = jnp.einsum("thn,hnl->thl", q_nope, key_up.astype(jnp.float32)).astype(jnp.bfloat16)
    q_lat32 = q_latent.astype(jnp.float32)
    latent32 = latent.astype(jnp.float32)
    new_latent = sample_new[:, :latent_width].astype(jnp.float32)
    new_rope = sample_new[:, latent_width:].astype(jnp.float32)
    prefix_scores = (jnp.einsum("thl,jl->thj", q_lat32, latent32)
                     + jnp.einsum("thr,rj->thj", q_rope, rotary.astype(jnp.float32))) * score_scale
    new_scores = (jnp.einsum("thl,ul->thu", q_lat32, new_latent)
                  + jnp.einsum("thr,ur->thu", q_rope, new_rope)) * score_scale
    step_count = sample_new.shape[0]
    visible = (jnp.arange(step_count)[None, :] <= jnp.arange(step_count)[:, None])[:, None, :]
    masked = jnp.where(visible, new_scores, -jnp.inf)
    row_max = jnp.maximum(jnp.max(prefix_scores, axis=2), jnp.max(masked, axis=2))
    prefix_exp = jnp.exp(prefix_scores - row_max[:, :, None])
    new_exp = jnp.where(visible, jnp.exp(masked - row_max[:, :, None]), 0.0)
    exp_total = jnp.sum(prefix_exp, axis=2) + jnp.sum(new_exp, axis=2)
    prefix_rounded = prefix_exp.astype(jnp.bfloat16).astype(jnp.float32)
    new_rounded = new_exp.astype(jnp.bfloat16).astype(jnp.float32)
    context = jnp.einsum("thj,jl->thl", prefix_rounded, latent32) + jnp.einsum("thu,ul->thl", new_rounded, new_latent)
    context = (context / exp_total[:, :, None]).astype(jnp.bfloat16)
    attended = jnp.einsum("thl,hlv->thv", context.astype(jnp.float32), value_up.astype(jnp.float32)).astype(jnp.bfloat16)
    return attended.reshape(step_count, -1)


def reference(queries, new_kv, owner_index, prefix_latent, prefix_rope, key_up, value_up, out_weight):
    latent = lax.dynamic_index_in_dim(prefix_latent, owner_index[0], 0, keepdims=False)
    rotary = lax.dynamic_index_in_dim(prefix_rope, owner_index[0], 0, keepdims=False)
    attended = lax.map(lambda pair: attend_sample(pair[0], pair[1], latent, rotary, key_up, value_up), (queries, new_kv))
    sample_count, step_count, flat_width = attended.shape
    layer_out = jnp.dot(attended.reshape(sample_count * step_count, flat_width), out_weight, preferred_element_type=jnp.float32)
    return layer_out.reshape(sample_count, step_count, -1).astype(jnp.bfloat16)
```

```python
import functools
import jax
import jax.numpy as jnp
from jax import lax
from jax.experimental import pallas as pl
from jax.experimental.pallas import tpu as pltpu
from jax.sharding import PartitionSpec as P

MESH = pl.DeviceIdType.MESH
BF = jnp.bfloat16


class Coord:
    def __init__(self):
        g, t = lax.axis_index("grp"), lax.axis_index("tp")
        self.x, self.y, self.z, self.c = g // 8, (g // 2) % 4, (g % 2) * 2 + t // 2, t % 2

    def at(self, **moved):
        x, y, z, c = (moved.get(k, getattr(self, k)) for k in "xyzc")
        return (x * 8 + y * 2 + z // 2, (z % 2) * 2 + c)


ORDERS = (("x", "y", "z"), ("y", "z", "x"), ("z", "x", "y"))
REGIONS = (
    (0, "A", 64, 0, 0),
    (0, "B", 32, 3, 0),
    (1, "A", 64, 1, 0),
    (1, "B", 32, 3, 4096),
    (2, "A", 64, 2, 0),
    (2, "R", 128, None, None),
)


def source_views(latent):
    return (
        latent.reshape(8, 4, 2, 2, 64, 512),
        latent.reshape(2, 8, 4, 2, 2, 32, 512),
        latent.reshape(8, 2, 2, 4, 64, 512),
        latent.reshape(2, 8, 2, 2, 4, 32, 512),
        latent.reshape(2, 2, 2, 4, 4, 64, 512),
    )


def landing_shapes():
    shapes = []
    for lane, kind, unit, _, _ in REGIONS:
        dims = ((4, 4, 2), (4, 2, 4), (2, 4, 4))[lane]
        for step in range(3):
            if kind == "R":
                width = unit
                for d in dims[step + 1 :]:
                    width *= d
                shapes.append(((dims[step], 32, width), (32, width)))
            else:
                tail = dims[step + 1 :] + (unit, 128)
                shapes.append(((dims[step],) + tail, tail))
    return shapes


def prefix_kernel(owner_ref, v0, v1, v2, v3, v4, rope_ref, lat_ref, rot_ref, *scratch):
    me = Coord()
    views = (v0, v1, v2, v3, v4, rope_ref)
    landings = [(scratch[2 * i], scratch[2 * i + 1]) for i in range(18)]
    sc_send, sc_recv, sc_own, ag_send, ag_recv, sw_send, sw_recv = scratch[36:]
    zh, zl = me.z // 2, me.z % 2
    owner = owner_ref[0]
    owner_digit = {"x": owner // 8, "y": (owner // 2) % 4, "z": owner % 2}

    barrier = pltpu.get_barrier_semaphore()
    peers = [me.at(**{a: (getattr(me, a) + d) % 4}) for a in "xyz" for d in (1, 2, 3)]
    peers.append(me.at(c=1 - me.c))
    for peer in peers:
        pl.semaphore_signal(barrier, inc=1, device_id=peer, device_id_type=MESH)
    pl.semaphore_wait(barrier, len(peers))

    def own_digit(axis):
        return zh if axis == "z" else getattr(me, axis)

    def source(region, digit):
        lane, kind, unit, tile, base = REGIONS[region]
        view = views[region]
        if kind == "R":
            start = pl.multiple_of(4096 * digit + 2048 * zl, 128)
            return view.at[pl.ds(pl.multiple_of(32 * me.c, 32), 32), pl.ds(start, 2048)]
        cols = pl.ds(tile * 128, 128)
        if lane == 2:
            return view.at[me.c, digit, zl, :, :, :, cols]
        lead = (lane,) if kind == "B" else ()
        if lane == 0:
            return view.at[lead + (me.c * 4 + digit, slice(None), slice(None), zl, slice(None), cols)]
        return view.at[lead + (me.c * 4 + digit, slice(None), zl, slice(None), slice(None), cols)]

    def part(region, step, digit):
        if step == 0:
            return source(region, digit)
        held = landings[region * 3 + step - 1][1]
        lane, kind, unit, tile, base = REGIONS[region]
        if kind == "R":
            width = landings[region * 3 + step][0].shape[2]
            return held.at[:, pl.ds(pl.multiple_of(digit * width, 128), width)]
        return held.at[digit]

    def scatter_copies(region, step):
        axis = ORDERS[REGIONS[region][0]][step]
        slots = landings[region * 3 + step][0]
        index = region * 3 + step
        mine = own_digit(axis)
        copies = []
        own = pltpu.make_async_copy(part(region, step, mine), slots.at[mine], sc_own.at[index])
        for d in (1, 2, 3) if axis != "z" else (2,):
            if axis == "z":
                target, digit = (me.z + 2) % 4, 1 - zh
            else:
                target = digit = (mine + d) % 4
            copies.append(
                pltpu.make_async_remote_copy(
                    src_ref=part(region, step, digit),
                    dst_ref=slots.at[mine],
                    send_sem=sc_send.at[index, d - 1],
                    recv_sem=sc_recv.at[index, d - 1],
                    device_id=me.at(**{axis: target}),
                    device_id_type=MESH,
                )
            )
        return own, copies

    def block(region, level, digits):
        lane, kind, unit, tile, base = REGIONS[region]
        count = unit * 4 ** (3 - level)
        place = 0
        for k in range(3):
            place = place * 4 + (digits[k] if k < level else 0)
        if kind == "R":
            start = pl.multiple_of(128 * place, 128)
            return rot_ref.at[pl.ds(pl.multiple_of(32 * me.c, 32), 32), pl.ds(start, count)]
        start = pl.multiple_of(base + unit * (64 * me.c + place), 32)
        return lat_ref.at[pl.ds(start, count), pl.ds(tile * 128, 128)]

    order = [ORDERS[r[0]] for r in REGIONS]
    digits = [tuple(getattr(me, a) for a in o) for o in order]
    pending = []
    started = []
    for region in range(6):
        own, copies = scatter_copies(region, 0)
        for copy in copies:
            copy.start()
        own.start()
        started.append((own, copies))
    for step in range(3):
        following = []
        for region in range(6):
            own, copies = started[region]
            own.wait()
            for copy in copies:
                copy.wait_recv()
            pending += copies
            axis = order[region][step]
            slots, held = landings[region * 3 + step]
            chosen = slots[owner_digit[axis]]
            if step < 2:
                held[...] = chosen
                own, copies = scatter_copies(region, step + 1)
                for copy in copies:
                    copy.start()
                own.start()
                following.append((own, copies))
            else:
                home = block(region, 3, digits[region])
                home[...] = chosen
                following.append(gather_start(region, 3, order, digits, me, block, ag_send, ag_recv))
        started = following

    swaps = []

    def swap(region, which, first):
        ref = block(region, 1, (first, 0, 0))
        copy = pltpu.make_async_remote_copy(
            src_ref=ref,
            dst_ref=ref,
            send_sem=sw_send.at[region, which],
            recv_sem=sw_recv.at[region, which],
            device_id=me.at(c=1 - me.c),
            device_id_type=MESH,
        )
        copy.start()
        swaps.append(copy)

    for level in (3, 2):
        following = []
        for region in range(6):
            for copy in started[region]:
                copy.wait_recv()
            pending += started[region]
            following.append(gather_start(region, level - 1, order, digits, me, block, ag_send, ag_recv))
            if level == 2:
                swap(region, 0, digits[region][0])
        started = following
    for d in (1, 2, 3):
        for region in range(6):
            started[region][d - 1].wait_recv()
            swap(region, d, (digits[region][0] + 4 - d) % 4)
    for region in range(6):
        pending += started[region]
    for copy in swaps:
        copy.wait_recv()
    for copy in pending + swaps:
        copy.wait_send()


def gather_start(region, level, order, digits, me, block, ag_send, ag_recv):
    axis = order[region][level - 1]
    ref = block(region, level, digits[region])
    copies = []
    for d in (1, 2, 3):
        copy = pltpu.make_async_remote_copy(
            src_ref=ref,
            dst_ref=ref,
            send_sem=ag_send.at[region, level - 1, d - 1],
            recv_sem=ag_recv.at[region, level - 1, d - 1],
            device_id=me.at(**{axis: (getattr(me, axis) + d) % 4}),
            device_id_type=MESH,
        )
        copy.start()
        copies.append(copy)
    return copies


def gather_prefix(owner_index, latent, rope):
    scratch = []
    for slots, held in landing_shapes():
        scratch += [pltpu.VMEM(slots, BF), pltpu.VMEM(held, BF)]
    sem = pltpu.SemaphoreType.DMA
    scratch += [sem((18, 3)), sem((18, 3)), sem((18,)), sem((6, 3, 3)), sem((6, 3, 3)), sem((6, 4)), sem((6, 4))]
    hbm = pl.BlockSpec(memory_space=pl.ANY)
    vmem = pl.BlockSpec(memory_space=pltpu.VMEM)
    return pl.pallas_call(
        prefix_kernel,
        out_shape=(jax.ShapeDtypeStruct((8192, 512), BF), jax.ShapeDtypeStruct((64, 8192), BF)),
        in_specs=[pl.BlockSpec(memory_space=pltpu.SMEM)] + [hbm] * 6,
        out_specs=(vmem, vmem),
        scratch_shapes=scratch,
        compiler_params=pltpu.CompilerParams(
            collective_id=0, has_side_effects=True, vmem_limit_bytes=48 << 20
        ),
        name="gather_prefix",
    )(owner_index, *source_views(latent), rope)


def body(queries, new_kv, owner_index, prefix_latent, prefix_rope, key_up, value_up, out_weight):
    samp_local, step_count, heads_local, query_width = queries.shape
    nope_width = key_up.shape[1]
    latent_width = key_up.shape[2]
    score_scale = query_width ** (-0.5)
    latent, rotary = gather_prefix(owner_index, prefix_latent[0], prefix_rope[0])
    q_nope = queries[:, :, :, :nope_width]
    q_rope = queries[:, :, :, nope_width:]
    q_latent = jnp.einsum(
        "sthn,hnl->sthl", q_nope, key_up, preferred_element_type=jnp.float32
    ).astype(jnp.bfloat16)
    row_count = samp_local * step_count * heads_local
    flat_latent = q_latent.reshape(row_count, latent_width)
    flat_rope = q_rope.reshape(row_count, query_width - nope_width)
    prefix_scores = lax.dot_general(
        flat_latent, latent, (((1,), (1,)), ((), ())), preferred_element_type=jnp.float32
    )
    prefix_scores = (
        prefix_scores + jnp.dot(flat_rope, rotary, preferred_element_type=jnp.float32)
    ) * score_scale
    new_latent = new_kv[:, :, :latent_width]
    new_rope = new_kv[:, :, latent_width:]
    new_scores = jnp.einsum(
        "sthl,sul->sthu", q_latent, new_latent, preferred_element_type=jnp.float32
    )
    new_scores = (
        new_scores
        + jnp.einsum("sthr,sur->sthu", q_rope, new_rope, preferred_element_type=jnp.float32)
    ) * score_scale
    visible = (jnp.arange(step_count)[None, :] <= jnp.arange(step_count)[:, None])[None, :, None, :]
    masked = jnp.where(visible, new_scores, -jnp.inf)
    row_max = jnp.maximum(
        jnp.max(prefix_scores, axis=1), jnp.max(masked, axis=3).reshape(row_count)
    )
    prefix_exp = jnp.exp(prefix_scores - row_max[:, None])
    new_exp = jnp.where(
        visible,
        jnp.exp(masked - row_max.reshape(samp_local, step_count, heads_local)[:, :, :, None]),
        0.0,
    )
    exp_total = jnp.sum(prefix_exp, axis=1) + jnp.sum(new_exp, axis=3).reshape(row_count)
    context = jnp.dot(prefix_exp.astype(jnp.bfloat16), latent, preferred_element_type=jnp.float32)
    new_context = jnp.einsum(
        "sthu,sul->sthl",
        new_exp.astype(jnp.bfloat16),
        new_latent,
        preferred_element_type=jnp.float32,
    )
    context = (context + new_context.reshape(row_count, latent_width)) / exp_total[:, None]
    context = context.astype(jnp.bfloat16).reshape(
        samp_local, step_count, heads_local, latent_width
    )
    attended = jnp.einsum(
        "sthl,hlv->sthv", context, value_up, preferred_element_type=jnp.float32
    ).astype(jnp.bfloat16)
    attended = attended.reshape(samp_local, step_count, -1)
    partial_terms = jnp.einsum(
        "stk,kd->std",
        lax.all_gather(attended, "grp", axis=0, tiled=True),
        out_weight,
        preferred_element_type=jnp.float32,
    )
    return lax.psum_scatter(
        partial_terms.astype(jnp.bfloat16), "tp", scatter_dimension=0, tiled=True
    )


def solution(mesh):
    return jax.shard_map(
        body,
        mesh=mesh,
        in_specs=(
            P("grp", None, "tp", None),
            P("grp", None, None),
            P(),
            P("grp", None, None),
            P("grp", None, None),
            P("tp", None, None),
            P("tp", None, None),
            P("tp", "grp"),
        ),
        out_specs=P("tp", None, "grp"),
        check_vma=False,
    )
```

```python
import functools
import jax
import jax.numpy as jnp
from jax import lax
from jax.experimental import pallas as pl
from jax.experimental.pallas import tpu as pltpu
from jax.sharding import PartitionSpec as P

MESH = pl.DeviceIdType.MESH
BF = jnp.bfloat16


class Coord:
    def __init__(self):
        g, t = lax.axis_index("grp"), lax.axis_index("tp")
        self.x, self.y, self.z, self.c = g // 8, (g // 2) % 4, (g % 2) * 2 + t // 2, t % 2

    def at(self, **moved):
        x, y, z, c = (moved.get(k, getattr(self, k)) for k in "xyzc")
        return (x * 8 + y * 2 + z // 2, (z % 2) * 2 + c)


ORDERS = (("x", "y", "z"), ("y", "z", "x"), ("z", "x", "y"))
REGIONS = (
    (0, "A", 64, 0, 0),
    (0, "B", 32, 3, 0),
    (1, "A", 64, 1, 0),
    (1, "B", 32, 3, 4096),
    (2, "A", 64, 2, 0),
    (2, "R", 128, None, None),
)


def source_views(latent):
    return (
        latent.reshape(8, 4, 2, 2, 64, 512),
        latent.reshape(2, 8, 4, 2, 2, 32, 512),
        latent.reshape(8, 2, 2, 4, 64, 512),
        latent.reshape(2, 8, 2, 2, 4, 32, 512),
        latent.reshape(2, 2, 2, 4, 4, 64, 512),
    )


def landing_shapes():
    shapes = []
    for lane, kind, unit, _, _ in REGIONS:
        dims = ((4, 4, 2), (4, 2, 4), (2, 4, 4))[lane]
        for step in range(3):
            if kind == "R":
                width = unit
                for d in dims[step + 1 :]:
                    width *= d
                shapes.append(((dims[step], 32, width), (32, width)))
            else:
                tail = dims[step + 1 :] + (unit, 128)
                shapes.append(((dims[step],) + tail, tail))
    return shapes


def layer_kernel(
    owner_ref, q_ref, new_ref, key_hbm, value_hbm, v0, v1, v2, v3, v4, rope_ref, att_ref,
    lat_ref, rot_ref, key_ref, value_ref, qlat_ref, acc_ref, max_ref, sum_ref, weight_sem, *scratch
):
    me = Coord()
    views = (v0, v1, v2, v3, v4, rope_ref)
    landings = [(scratch[2 * i], scratch[2 * i + 1]) for i in range(18)]
    sc_send, sc_recv, sc_own, ag_send, ag_recv, sw_send, sw_recv = scratch[36:]
    key_copy = pltpu.make_async_copy(key_hbm, key_ref, weight_sem.at[0])
    value_copy = pltpu.make_async_copy(value_hbm, value_ref, weight_sem.at[1])
    zh, zl = me.z // 2, me.z % 2
    owner = owner_ref[0]
    owner_digit = {"x": owner // 8, "y": (owner // 2) % 4, "z": owner % 2}

    barrier = pltpu.get_barrier_semaphore()
    peers = [me.at(**{a: (getattr(me, a) + d) % 4}) for a in "xyz" for d in (1, 2, 3)]
    peers.append(me.at(c=1 - me.c))
    for peer in peers:
        pl.semaphore_signal(barrier, inc=1, device_id=peer, device_id_type=MESH)
    pl.semaphore_wait(barrier, len(peers))

    def own_digit(axis):
        return zh if axis == "z" else getattr(me, axis)

    def source(region, digit):
        lane, kind, unit, tile, base = REGIONS[region]
        view = views[region]
        if kind == "R":
            start = pl.multiple_of(4096 * digit + 2048 * zl, 128)
            return view.at[pl.ds(pl.multiple_of(32 * me.c, 32), 32), pl.ds(start, 2048)]
        cols = pl.ds(tile * 128, 128)
        if lane == 2:
            return view.at[me.c, digit, zl, :, :, :, cols]
        lead = (lane,) if kind == "B" else ()
        if lane == 0:
            return view.at[lead + (me.c * 4 + digit, slice(None), slice(None), zl, slice(None), cols)]
        return view.at[lead + (me.c * 4 + digit, slice(None), zl, slice(None), slice(None), cols)]

    def part(region, step, digit):
        if step == 0:
            return source(region, digit)
        held = landings[region * 3 + step - 1][1]
        lane, kind, unit, tile, base = REGIONS[region]
        if kind == "R":
            width = landings[region * 3 + step][0].shape[2]
            return held.at[:, pl.ds(pl.multiple_of(digit * width, 128), width)]
        return held.at[digit]

    def scatter_copies(region, step):
        axis = ORDERS[REGIONS[region][0]][step]
        slots = landings[region * 3 + step][0]
        index = region * 3 + step
        mine = own_digit(axis)
        copies = []
        own = pltpu.make_async_copy(part(region, step, mine), slots.at[mine], sc_own.at[index])
        for d in (1, 2, 3) if axis != "z" else (2,):
            if axis == "z":
                target, digit = (me.z + 2) % 4, 1 - zh
            else:
                target = digit = (mine + d) % 4
            copies.append(
                pltpu.make_async_remote_copy(
                    src_ref=part(region, step, digit),
                    dst_ref=slots.at[mine],
                    send_sem=sc_send.at[index, d - 1],
                    recv_sem=sc_recv.at[index, d - 1],
                    device_id=me.at(**{axis: target}),
                    device_id_type=MESH,
                )
            )
        return own, copies

    def block(region, level, digits):
        lane, kind, unit, tile, base = REGIONS[region]
        count = unit * 4 ** (3 - level)
        place = 0
        for k in range(3):
            place = place * 4 + (digits[k] if k < level else 0)
        if kind == "R":
            start = pl.multiple_of(128 * place, 128)
            return rot_ref.at[pl.ds(pl.multiple_of(32 * me.c, 32), 32), pl.ds(start, count)]
        start = pl.multiple_of(base + unit * (64 * me.c + place), 32)
        return lat_ref.at[pl.ds(start, count), pl.ds(tile * 128, 128)]

    order = [ORDERS[r[0]] for r in REGIONS]
    digits = [tuple(getattr(me, a) for a in o) for o in order]
    pending = []
    started = []
    for region in range(6):
        own, copies = scatter_copies(region, 0)
        for copy in copies:
            copy.start()
        own.start()
        started.append((own, copies))
    key_copy.start()
    value_copy.start()
    key_copy.wait()
    latent_queries(q_ref, key_ref, qlat_ref)
    new_keys(q_ref, new_ref, qlat_ref, acc_ref, max_ref, sum_ref)
    for step in range(3):
        following = []
        for region in range(6):
            own, copies = started[region]
            own.wait()
            for copy in copies:
                copy.wait_recv()
            pending += copies
            axis = order[region][step]
            slots, held = landings[region * 3 + step]
            chosen = slots[owner_digit[axis]]
            if step < 2:
                held[...] = chosen
                own, copies = scatter_copies(region, step + 1)
                for copy in copies:
                    copy.start()
                own.start()
                following.append((own, copies))
            else:
                home = block(region, 3, digits[region])
                home[...] = chosen
                following.append(gather_start(region, 3, order, digits, me, block, ag_send, ag_recv))
        started = following

    swaps = []

    def swap(region, which, first):
        ref = block(region, 1, (first, 0, 0))
        copy = pltpu.make_async_remote_copy(
            src_ref=ref,
            dst_ref=ref,
            send_sem=sw_send.at[region, which],
            recv_sem=sw_recv.at[region, which],
            device_id=me.at(c=1 - me.c),
            device_id_type=MESH,
        )
        copy.start()
        swaps.append(copy)

    for level in (3, 2):
        following = []
        for region in range(6):
            for copy in started[region]:
                copy.wait_recv()
            pending += started[region]
            following.append(gather_start(region, level - 1, order, digits, me, block, ag_send, ag_recv))
            if level == 2:
                swap(region, 0, digits[region][0])
        started = following
    for d in (1, 2, 3):
        for region in range(6):
            started[region][d - 1].wait_recv()
            swap(region, d, (digits[region][0] + 4 - d) % 4)
    for region in range(6):
        pending += started[region]
    for copy in swaps:
        copy.wait_recv()
    for copy in pending + swaps:
        copy.wait_send()

    prefix_keys(q_ref, qlat_ref, lat_ref, rot_ref, acc_ref, max_ref, sum_ref)
    value_copy.wait()
    attended_values(acc_ref, sum_ref, value_ref, att_ref)


SCALE = 192**-0.5 * 1.4426950408889634
LAST = (((1,), (1,)), ((), ()))
ROWS = 512
KEYS = 1024


def dot(a, b):
    return jnp.dot(a, b, preferred_element_type=jnp.float32)


def dot_last(a, b):
    return lax.dot_general(a, b, LAST, preferred_element_type=jnp.float32)


def latent_queries(q_ref, key_ref, qlat_ref):
    @pl.loop(0, 32, unroll=4)
    def _(h):
        rows = pl.ds(pl.multiple_of(h * 32, 32), 32)
        qlat_ref[rows, :] = dot(q_ref[rows, 0:128], key_ref[h]).astype(BF)


def new_keys(q_ref, new_ref, qlat_ref, acc_ref, max_ref, sum_ref):
    @pl.loop(0, 1024 // ROWS)
    def _(r):
        rows = pl.ds(pl.multiple_of(r * ROWS, ROWS), ROWS)
        scores = dot_last(qlat_ref[rows, :], new_ref[:, 0:512])
        scores = (scores + dot_last(q_ref[rows, 128:192], new_ref[:, 512:576])) * SCALE
        row = lax.broadcasted_iota(jnp.int32, (ROWS, 32), 0) % 32
        key = lax.broadcasted_iota(jnp.int32, (ROWS, 32), 1)
        visible = (row // 4 == key // 4) & (key <= row)
        top = jnp.max(jnp.where(visible, scores, -jnp.inf), axis=1, keepdims=True)
        e = jnp.where(visible, jnp.exp2(jnp.where(visible, scores, top) - top), 0.0)
        max_ref[rows, :] = jnp.broadcast_to(top, (ROWS, 128))
        sum_ref[rows, :] = jnp.broadcast_to(jnp.sum(e, axis=1, keepdims=True), (ROWS, 128))
        acc_ref[rows, :] = dot(e.astype(BF), new_ref[:, 0:512])


def prefix_keys(q_ref, qlat_ref, lat_ref, rot_ref, acc_ref, max_ref, sum_ref):
    @pl.loop(0, 8192 // KEYS)
    def _(k):
        keys = pl.ds(pl.multiple_of(k * KEYS, KEYS), KEYS)
        blocks = [pl.ds(r * ROWS, ROWS) for r in range(1024 // ROWS)]
        scores = [
            dot_last(qlat_ref[rows, :], lat_ref[keys, :]) + dot(q_ref[rows, 128:192], rot_ref[:, keys])
            for rows in blocks
        ]
        for rows, s in zip(blocks, scores):
            old = max_ref[rows, :]
            new = jnp.maximum(old, jnp.max(s, axis=1, keepdims=True) * SCALE)
            max_ref[rows, :] = new
            shrink = jnp.exp2(old - new)
            e = jnp.exp2(s * SCALE - new[:, 0:1])
            sum_ref[rows, :] = sum_ref[rows, :] * shrink + jnp.sum(e, axis=1, keepdims=True)
            acc_ref[rows, :] = acc_ref[rows, :] * shrink[:, 0:1] + dot(e.astype(BF), lat_ref[keys, :])


def attended_values(acc_ref, sum_ref, value_ref, att_ref):
    @pl.loop(0, 32, unroll=4)
    def _(h):
        rows = pl.ds(pl.multiple_of(h * 32, 32), 32)
        context = (acc_ref[rows, :] / sum_ref[rows, 0:1]).astype(BF)
        cols = pl.ds(pl.multiple_of(h * 128, 128), 128)
        att_ref[:, cols] = dot(context, value_ref[h]).astype(BF)


def gather_start(region, level, order, digits, me, block, ag_send, ag_recv):
    axis = order[region][level - 1]
    ref = block(region, level, digits[region])
    copies = []
    for d in (1, 2, 3):
        copy = pltpu.make_async_remote_copy(
            src_ref=ref,
            dst_ref=ref,
            send_sem=ag_send.at[region, level - 1, d - 1],
            recv_sem=ag_recv.at[region, level - 1, d - 1],
            device_id=me.at(**{axis: (getattr(me, axis) + d) % 4}),
            device_id_type=MESH,
        )
        copy.start()
        copies.append(copy)
    return copies


def attend(owner_index, queries, new_kv, key_up, value_up, latent, rope):
    scratch = [
        pltpu.VMEM((8192, 512), BF),
        pltpu.VMEM((64, 8192), BF),
        pltpu.VMEM((32, 128, 512), BF),
        pltpu.VMEM((32, 512, 128), BF),
        pltpu.VMEM((1024, 512), BF),
        pltpu.VMEM((1024, 512), jnp.float32),
        pltpu.VMEM((1024, 128), jnp.float32),
        pltpu.VMEM((1024, 128), jnp.float32),
        pltpu.SemaphoreType.DMA((2,)),
    ]
    for slots, held in landing_shapes():
        scratch += [pltpu.VMEM(slots, BF), pltpu.VMEM(held, BF)]
    sem = pltpu.SemaphoreType.DMA
    scratch += [sem((18, 3)), sem((18, 3)), sem((18,)), sem((6, 3, 3)), sem((6, 3, 3)), sem((6, 4)), sem((6, 4))]
    hbm = pl.BlockSpec(memory_space=pl.ANY)
    vmem = pl.BlockSpec(memory_space=pltpu.VMEM)
    return pl.pallas_call(
        layer_kernel,
        out_shape=jax.ShapeDtypeStruct((32, 4096), BF),
        in_specs=[pl.BlockSpec(memory_space=pltpu.SMEM), vmem, vmem] + [hbm] * 8,
        out_specs=vmem,
        scratch_shapes=scratch,
        compiler_params=pltpu.CompilerParams(
            collective_id=0, has_side_effects=True, vmem_limit_bytes=60 << 20
        ),
        name="attend",
    )(owner_index, queries, new_kv, key_up, value_up, *source_views(latent), rope)


def body(queries, new_kv, owner_index, prefix_latent, prefix_rope, key_up, value_up, out_weight):
    samples, steps, heads, width = queries.shape
    rows = jnp.transpose(queries, (2, 0, 1, 3)).reshape(heads * samples * steps, width)
    attended = attend(
        owner_index, rows, new_kv.reshape(samples * steps, -1), key_up, value_up, prefix_latent[0], prefix_rope[0]
    )
    partial_terms = jnp.einsum(
        "stk,kd->std",
        lax.all_gather(attended.reshape(samples, steps, -1), "grp", axis=0, tiled=True),
        out_weight,
        preferred_element_type=jnp.float32,
    )
    return lax.psum_scatter(
        partial_terms.astype(jnp.bfloat16), "tp", scatter_dimension=0, tiled=True
    )


def solution(mesh):
    return jax.shard_map(
        body,
        mesh=mesh,
        in_specs=(
            P("grp", None, "tp", None),
            P("grp", None, None),
            P(),
            P("grp", None, None),
            P("grp", None, None),
            P("tp", None, None),
            P("tp", None, None),
            P("tp", "grp"),
        ),
        out_specs=P("tp", None, "grp"),
        check_vma=False,
    )
```

```python
import functools
import jax
import jax.numpy as jnp
from jax import lax
from jax.experimental import pallas as pl
from jax.experimental.pallas import tpu as pltpu
from jax.sharding import PartitionSpec as P

MESH = pl.DeviceIdType.MESH
BF = jnp.bfloat16


class Coord:
    def __init__(self):
        g, t = lax.axis_index("grp"), lax.axis_index("tp")
        self.x, self.y, self.z, self.c = g // 8, (g // 2) % 4, (g % 2) * 2 + t // 2, t % 2

    def at(self, **moved):
        x, y, z, c = (moved.get(k, getattr(self, k)) for k in "xyzc")
        return (x * 8 + y * 2 + z // 2, (z % 2) * 2 + c)


ORDERS = (("x", "y", "z"), ("y", "z", "x"), ("z", "x", "y"))
REGIONS = (
    (0, "A", 64, 0, 0),
    (0, "B", 32, 3, 0),
    (1, "A", 64, 1, 0),
    (1, "B", 32, 3, 4096),
    (2, "A", 64, 2, 0),
    (2, "R", 128, None, None),
)


def source_views(latent):
    return (
        latent.reshape(8, 4, 2, 2, 64, 512),
        latent.reshape(2, 8, 4, 2, 2, 32, 512),
        latent.reshape(8, 2, 2, 4, 64, 512),
        latent.reshape(2, 8, 2, 2, 4, 32, 512),
        latent.reshape(2, 2, 2, 4, 4, 64, 512),
    )


def landing_shapes():
    shapes = []
    for lane, kind, unit, _, _ in REGIONS:
        dims = ((4, 4, 2), (4, 2, 4), (2, 4, 4))[lane]
        for step in range(3):
            if kind == "R":
                width = unit
                for d in dims[step + 1 :]:
                    width *= d
                shapes.append(((dims[step], 32, width), (32, width)))
            else:
                tail = dims[step + 1 :] + (unit, 128)
                shapes.append(((dims[step],) + tail, tail))
    return shapes


def layer_kernel(
    owner_ref, q_ref, new_ref, key_hbm, value_hbm, weight_hbm, v0, v1, v2, v3, v4, rope_ref, out_ref,
    lat_ref, rot_ref, key_ref, value_ref, weight_ref, qlat_ref, score_ref, acc_ref, max_ref, sum_ref,
    att_ref, total_ref, part_ref, weight_sem, ex_send, ex_recv, rs_send, rs_recv, *scratch
):
    me = Coord()
    views = (v0, v1, v2, v3, v4, rope_ref)
    landings = [(scratch[2 * i], scratch[2 * i + 1]) for i in range(18)]
    sc_send, sc_recv, sc_own, ag_send, ag_recv, sw_send, sw_recv = scratch[36:]
    key_copy = pltpu.make_async_copy(key_hbm, key_ref, weight_sem.at[0])
    value_copy = pltpu.make_async_copy(value_hbm, value_ref, weight_sem.at[1])
    weight_copy = pltpu.make_async_copy(weight_hbm, weight_ref, weight_sem.at[2])
    zh, zl = me.z // 2, me.z % 2
    owner = owner_ref[0]
    owner_digit = {"x": owner // 8, "y": (owner // 2) % 4, "z": owner % 2}

    barrier = pltpu.get_barrier_semaphore()
    peers = [me.at(**{a: (getattr(me, a) + d) % 4}) for a in "xyz" for d in (1, 2, 3)]
    z_mate = me.z + 1 - 2 * zl
    peers += [me.at(c=1 - me.c), me.at(z=z_mate, c=1 - me.c)]
    for peer in peers:
        pl.semaphore_signal(barrier, inc=1, device_id=peer, device_id_type=MESH)
    pl.semaphore_wait(barrier, len(peers))

    def own_digit(axis):
        return zh if axis == "z" else getattr(me, axis)

    def source(region, digit):
        lane, kind, unit, tile, base = REGIONS[region]
        view = views[region]
        if kind == "R":
            start = pl.multiple_of(4096 * digit + 2048 * zl, 128)
            return view.at[pl.ds(pl.multiple_of(32 * me.c, 32), 32), pl.ds(start, 2048)]
        cols = pl.ds(tile * 128, 128)
        if lane == 2:
            return view.at[me.c, digit, zl, :, :, :, cols]
        lead = (lane,) if kind == "B" else ()
        if lane == 0:
            return view.at[lead + (me.c * 4 + digit, slice(None), slice(None), zl, slice(None), cols)]
        return view.at[lead + (me.c * 4 + digit, slice(None), zl, slice(None), slice(None), cols)]

    def part(region, step, digit):
        if step == 0:
            return source(region, digit)
        held = landings[region * 3 + step - 1][1]
        lane, kind, unit, tile, base = REGIONS[region]
        if kind == "R":
            width = landings[region * 3 + step][0].shape[2]
            return held.at[:, pl.ds(pl.multiple_of(digit * width, 128), width)]
        return held.at[digit]

    def scatter_copies(region, step):
        axis = ORDERS[REGIONS[region][0]][step]
        slots = landings[region * 3 + step][0]
        index = region * 3 + step
        mine = own_digit(axis)
        copies = []
        own = pltpu.make_async_copy(part(region, step, mine), slots.at[mine], sc_own.at[index])
        for d in (1, 2, 3) if axis != "z" else (2,):
            if axis == "z":
                target, digit = (me.z + 2) % 4, 1 - zh
            else:
                target = digit = (mine + d) % 4
            copies.append(
                pltpu.make_async_remote_copy(
                    src_ref=part(region, step, digit),
                    dst_ref=slots.at[mine],
                    send_sem=sc_send.at[index, d - 1],
                    recv_sem=sc_recv.at[index, d - 1],
                    device_id=me.at(**{axis: target}),
                    device_id_type=MESH,
                )
            )
        return own, copies

    def block(region, level, digits):
        lane, kind, unit, tile, base = REGIONS[region]
        count = unit * 4 ** (3 - level)
        place = 0
        for k in range(3):
            place = place * 4 + (digits[k] if k < level else 0)
        if kind == "R":
            start = pl.multiple_of(128 * place, 128)
            return rot_ref.at[pl.ds(pl.multiple_of(32 * me.c, 32), 32), pl.ds(start, count)]
        start = pl.multiple_of(base + unit * (64 * me.c + place), 32)
        return lat_ref.at[pl.ds(start, count), pl.ds(tile * 128, 128)]

    order = [ORDERS[r[0]] for r in REGIONS]
    digits = [tuple(getattr(me, a) for a in o) for o in order]
    pending = []
    started = []
    for region in range(6):
        own, copies = scatter_copies(region, 0)
        for copy in copies:
            copy.start()
        own.start()
        started.append((own, copies))
    key_copy.start()
    value_copy.start()
    weight_copy.start()
    key_copy.wait()
    latent_queries(q_ref, key_ref, qlat_ref)
    new_keys(q_ref, new_ref, qlat_ref, acc_ref, max_ref, sum_ref)
    for step in range(3):
        following = []
        for region in range(6):
            own, copies = started[region]
            own.wait()
            for copy in copies:
                copy.wait_recv()
            pending += copies
            axis = order[region][step]
            slots, held = landings[region * 3 + step]
            chosen = slots[owner_digit[axis]]
            if step < 2:
                held[...] = chosen
                own, copies = scatter_copies(region, step + 1)
                for copy in copies:
                    copy.start()
                own.start()
                following.append((own, copies))
            else:
                home = block(region, 3, digits[region])
                home[...] = chosen
                following.append(gather_start(region, 3, order, digits, me, block, ag_send, ag_recv))
        started = following

    swaps = []

    def swap(region, which, first):
        ref = block(region, 1, (first, 0, 0))
        copy = pltpu.make_async_remote_copy(
            src_ref=ref,
            dst_ref=ref,
            send_sem=sw_send.at[region, which],
            recv_sem=sw_recv.at[region, which],
            device_id=me.at(c=1 - me.c),
            device_id_type=MESH,
        )
        copy.start()
        swaps.append(copy)

    for level in (3, 2):
        following = []
        for region in range(6):
            for copy in started[region]:
                copy.wait_recv()
            pending += started[region]
            following.append(gather_start(region, level - 1, order, digits, me, block, ag_send, ag_recv))
            if level == 2:
                swap(region, 0, digits[region][0])
        started = following
    for d in (1, 2, 3):
        for region in range(6):
            started[region][d - 1].wait_recv()
            swap(region, d, (digits[region][0] + 4 - d) % 4)
    for region in range(6):
        pending += started[region]
    for copy in swaps:
        copy.wait_recv()
    pending += swaps

    def exchange(chunk):
        for step in range(3):
            copies = []
            for lane, (low, high) in enumerate(EX_LANES):
                axis = EX_ORDERS[lane][step]
                done = EX_ORDERS[lane][:step]
                cols = pl.ds(chunk * CHUNK + low, high - low)
                where = tuple(
                    slice(None) if a in done else d for a, d in (("x", me.x), ("y", me.y), ("z", zh))
                )
                ref = att_ref.at[where + (slice(None), cols)]
                for d in (1, 2, 3) if axis != "z" else (2,):
                    copy = pltpu.make_async_remote_copy(
                        src_ref=ref,
                        dst_ref=ref,
                        send_sem=ex_send.at[chunk, lane * 3 + step, d - 1],
                        recv_sem=ex_recv.at[chunk, lane * 3 + step, d - 1],
                        device_id=me.at(**{axis: (getattr(me, axis) + d) % 4}),
                        device_id_type=MESH,
                    )
                    copy.start()
                    copies.append(copy)
            yield
            for copy in copies:
                copy.wait_recv()
            pending.extend(copies)

    def partial_out(chunk, block):
        cols = pl.ds(chunk * CHUNK, CHUNK)
        values = att_ref[block, :, :, :, cols].reshape(256, CHUNK)
        return dot_last(values, weight_ref[:, cols])

    active = []
    for chunk in range(CHUNKS):
        for piece in range(2):
            prefix_keys(chunk * ROWS, piece * 4, 4, q_ref, qlat_ref, lat_ref, rot_ref, score_ref, acc_ref, max_ref, sum_ref)
            for steps in active:
                if steps[0] < 3:
                    next(steps[1])
                    steps[0] += 1
        if chunk == 0:
            value_copy.wait()
        attended_values(chunk, acc_ref, sum_ref, value_ref, att_ref, (me.x, me.y, zh))
        active.append([1, exchange(chunk)])
        next(active[-1][1])
    weight_copy.wait()
    for chunk in range(CHUNKS - 1):
        for steps in active[chunk:]:
            if steps[0] < 3 and steps is not active[chunk]:
                next(steps[1])
                steps[0] += 1
        for _ in active[chunk][1]:
            pass
        @pl.loop(0, 4)
        def _(block):
            term = partial_out(chunk, block)
            total_ref[block] = term if chunk == 0 else total_ref[block] + term
    for _ in active[-1][1]:
        pass
    tp = zl * 2 + me.c
    for d, (flip_z, flip_c) in enumerate(((1, 1), (1, 0), (0, 1), (0, 0))):
        target_z = z_mate if flip_z else me.z
        target_c = 1 - me.c if flip_c else me.c
        block = (target_z % 2) * 2 + target_c
        term = total_ref[block] + partial_out(CHUNKS - 1, block)
        if d == 3:
            total_ref[block] = term
            continue
        part_ref[d] = term.astype(BF)
        copy = pltpu.make_async_remote_copy(
            src_ref=part_ref.at[d],
            dst_ref=part_ref.at[3 + d],
            send_sem=rs_send.at[d],
            recv_sem=rs_recv.at[d],
            device_id=me.at(z=target_z, c=target_c),
            device_id_type=MESH,
        )
        copy.start()
        pending.append(copy)
    result = total_ref[tp]
    for d, copy in enumerate(pending[-3:]):
        copy.wait_recv()
        result = result + part_ref[3 + d].astype(jnp.float32)
    out_ref[...] = result.astype(BF)
    for copy in pending:
        copy.wait_send()


CHUNKS = 4
CHUNK = 4096 // CHUNKS
EX_ORDERS = (("z", "y", "x"), ("x", "z", "y"), ("y", "x", "z"))
EX_LANES = ((0, 256), (256, 640), (640, 1024))
SCALE = 192**-0.5 * 1.4426950408889634
LAST = (((1,), (1,)), ((), ()))
ROWS = 1024 // CHUNKS
KEYS = 1024


def dot(a, b):
    return jnp.dot(a, b, preferred_element_type=jnp.float32)


def dot_last(a, b):
    return lax.dot_general(a, b, LAST, preferred_element_type=jnp.float32)


def latent_queries(q_ref, key_ref, qlat_ref):
    @pl.loop(0, 32, unroll=4)
    def _(h):
        rows = pl.ds(pl.multiple_of(h * 32, 32), 32)
        qlat_ref[rows, :] = dot(q_ref[rows, 0:128], key_ref[h]).astype(BF)


def new_keys(q_ref, new_ref, qlat_ref, acc_ref, max_ref, sum_ref):
    @pl.loop(0, 1024 // ROWS)
    def _(r):
        rows = pl.ds(pl.multiple_of(r * ROWS, ROWS), ROWS)
        scores = dot_last(qlat_ref[rows, :], new_ref[:, 0:512])
        scores = (scores + dot_last(q_ref[rows, 128:192], new_ref[:, 512:576])) * SCALE
        row = lax.broadcasted_iota(jnp.int32, (ROWS, 32), 0) % 32
        key = lax.broadcasted_iota(jnp.int32, (ROWS, 32), 1)
        visible = (row // 4 == key // 4) & (key <= row)
        top = jnp.max(jnp.where(visible, scores, -jnp.inf), axis=1, keepdims=True)
        e = jnp.where(visible, jnp.exp2(jnp.where(visible, scores, top) - top), 0.0)
        max_ref[rows, :] = jnp.broadcast_to(top, (ROWS, 128))
        sum_ref[rows, :] = jnp.broadcast_to(jnp.sum(e, axis=1, keepdims=True), (ROWS, 128))
        acc_ref[rows, :] = dot(e.astype(BF), new_ref[:, 0:512])


def prefix_keys(row, first, count, q_ref, qlat_ref, lat_ref, rot_ref, score_ref, acc_ref, max_ref, sum_ref):
    rows = pl.ds(row, ROWS)

    def scores(k):
        keys = pl.ds(pl.multiple_of(k * KEYS, KEYS), KEYS)
        return dot_last(qlat_ref[rows, :], lat_ref[keys, :]) + dot(q_ref[rows, 128:192], rot_ref[:, keys])

    def take(k, s):
        keys = pl.ds(pl.multiple_of(k * KEYS, KEYS), KEYS)
        old = max_ref[rows, :]
        new = jnp.maximum(old, jnp.max(s, axis=1, keepdims=True) * SCALE)
        max_ref[rows, :] = new
        shrink = jnp.exp2(old - new)
        e = jnp.exp2(s * SCALE - new[:, 0:1])
        sum_ref[rows, :] = sum_ref[rows, :] * shrink + jnp.sum(e, axis=1, keepdims=True)
        acc_ref[rows, :] = acc_ref[rows, :] * shrink[:, 0:1] + dot(e.astype(BF), lat_ref[keys, :])

    if first == 0:
        score_ref[0] = scores(0)

    @pl.loop(first // 2, (first + count) // 2)
    def _(pair):
        k = pair * 2
        s = score_ref[0]
        score_ref[1] = scores(k + 1)
        take(k, s)
        s = score_ref[1]
        score_ref[0] = scores(jnp.minimum(k + 2, 8192 // KEYS - 1))
        take(k + 1, s)


def attended_values(chunk, acc_ref, sum_ref, value_ref, att_ref, place):
    heads = 32 // CHUNKS

    @pl.loop(chunk * heads, (chunk + 1) * heads, unroll=4)
    def _(h):
        rows = pl.ds(pl.multiple_of(h * 32, 32), 32)
        context = (acc_ref[rows, :] / sum_ref[rows, 0:1]).astype(BF)
        cols = pl.ds(pl.multiple_of(h * 128, 128), 128)
        att_ref[place + (slice(None), cols)] = dot(context, value_ref[h]).astype(BF)


def gather_start(region, level, order, digits, me, block, ag_send, ag_recv):
    axis = order[region][level - 1]
    ref = block(region, level, digits[region])
    copies = []
    for d in (1, 2, 3):
        copy = pltpu.make_async_remote_copy(
            src_ref=ref,
            dst_ref=ref,
            send_sem=ag_send.at[region, level - 1, d - 1],
            recv_sem=ag_recv.at[region, level - 1, d - 1],
            device_id=me.at(**{axis: (getattr(me, axis) + d) % 4}),
            device_id_type=MESH,
        )
        copy.start()
        copies.append(copy)
    return copies


def layer(owner_index, queries, new_kv, key_up, value_up, out_weight, latent, rope):
    sem = pltpu.SemaphoreType.DMA
    f32 = jnp.float32
    scratch = [
        pltpu.VMEM((8192, 512), BF),
        pltpu.VMEM((64, 8192), BF),
        pltpu.VMEM((32, 128, 512), BF),
        pltpu.VMEM((32, 512, 128), BF),
        pltpu.VMEM((224, 4096), BF),
        pltpu.VMEM((1024, 512), BF),
        pltpu.VMEM((2, ROWS, KEYS), f32),
        pltpu.VMEM((1024, 512), f32),
        pltpu.VMEM((1024, 128), f32),
        pltpu.VMEM((1024, 128), f32),
        pltpu.VMEM((4, 4, 2, 32, 4096), BF),
        pltpu.VMEM((4, 256, 224), f32),
        pltpu.VMEM((6, 256, 224), BF),
        sem((3,)),
        sem((CHUNKS, 9, 3)),
        sem((CHUNKS, 9, 3)),
        sem((3,)),
        sem((3,)),
    ]
    for slots, held in landing_shapes():
        scratch += [pltpu.VMEM(slots, BF), pltpu.VMEM(held, BF)]
    scratch += [sem((18, 3)), sem((18, 3)), sem((18,)), sem((6, 3, 3)), sem((6, 3, 3)), sem((6, 4)), sem((6, 4))]
    hbm = pl.BlockSpec(memory_space=pl.ANY)
    vmem = pl.BlockSpec(memory_space=pltpu.VMEM)
    return pl.pallas_call(
        layer_kernel,
        out_shape=jax.ShapeDtypeStruct((256, 224), BF),
        in_specs=[pl.BlockSpec(memory_space=pltpu.SMEM), vmem, vmem] + [hbm] * 9,
        out_specs=vmem,
        scratch_shapes=scratch,
        compiler_params=pltpu.CompilerParams(
            collective_id=0, has_side_effects=True, vmem_limit_bytes=60 << 20
        ),
        name="layer",
    )(owner_index, queries, new_kv, key_up, value_up, out_weight, *source_views(latent), rope)


def body(queries, new_kv, owner_index, prefix_latent, prefix_rope, key_up, value_up, out_weight):
    samples, steps, heads, width = queries.shape
    rows = jnp.transpose(queries.reshape(samples * steps, heads, width), (1, 0, 2)).reshape(-1, width)
    out = layer(
        owner_index, rows, new_kv.reshape(samples * steps, -1), key_up, value_up, out_weight.T, prefix_latent[0], prefix_rope[0]
    )
    return out.reshape(64, steps, -1)


def solution(mesh):
    return jax.shard_map(
        body,
        mesh=mesh,
        in_specs=(
            P("grp", None, "tp", None),
            P("grp", None, None),
            P(),
            P("grp", None, None),
            P("grp", None, None),
            P("tp", None, None),
            P("tp", None, None),
            P("tp", "grp"),
        ),
        out_specs=P("tp", None, "grp"),
        check_vma=False,
    )
```

```python
import functools
import jax
import jax.numpy as jnp
from jax import lax
from jax.experimental import pallas as pl
from jax.experimental.pallas import tpu as pltpu
from jax.sharding import PartitionSpec as P

MESH = pl.DeviceIdType.MESH
BF = jnp.bfloat16


class Coord:
    def __init__(self):
        g, t = lax.axis_index("grp"), lax.axis_index("tp")
        self.x, self.y, self.z, self.c = g // 8, (g // 2) % 4, (g % 2) * 2 + t // 2, t % 2

    def at(self, **moved):
        x, y, z, c = (moved.get(k, getattr(self, k)) for k in "xyzc")
        return (x * 8 + y * 2 + z // 2, (z % 2) * 2 + c)


ORDERS = (("x", "y", "z"), ("y", "z", "x"), ("z", "x", "y"))
REGIONS = (
    (0, "A", 64, 0, 0),
    (0, "B", 32, 3, 0),
    (1, "A", 64, 1, 0),
    (1, "B", 32, 3, 4096),
    (2, "A", 64, 2, 0),
    (2, "R", 128, None, None),
)


def source_views(latent):
    return (
        latent.reshape(8, 4, 2, 2, 64, 512),
        latent.reshape(2, 8, 4, 2, 2, 32, 512),
        latent.reshape(8, 2, 2, 4, 64, 512),
        latent.reshape(2, 8, 2, 2, 4, 32, 512),
        latent.reshape(2, 2, 2, 4, 4, 64, 512),
    )


def landing_shapes():
    shapes = []
    for lane, kind, unit, _, _ in REGIONS:
        dims = ((4, 4, 2), (4, 2, 4), (2, 4, 4))[lane]
        for step in range(3):
            if kind == "R":
                width = unit
                for d in dims[step + 1 :]:
                    width *= d
                shapes.append(((dims[step], 32, width), (32, width)))
            else:
                tail = dims[step + 1 :] + (unit, 128)
                shapes.append(((dims[step],) + tail, tail))
    return shapes


def layer_kernel(
    owner_ref, q_ref, new_ref, key_hbm, value_hbm, weight_hbm, v0, v1, v2, v3, v4, rope_ref, out_ref,
    lat_ref, rot_ref, key_ref, value_ref, weight_ref, qlat_ref, score_ref, acc_ref, max_ref, sum_ref,
    att_ref, total_ref, part_ref, land_ref, weight_sem, ex_send, ex_recv, rs_send, rs_recv, *scratch
):
    me = Coord()
    views = (v0, v1, v2, v3, v4, rope_ref)
    landings = [(scratch[2 * i], scratch[2 * i + 1]) for i in range(18)]
    sc_send, sc_recv, sc_own, ag_send, ag_recv, sw_send, sw_recv = scratch[36:]
    key_copy = pltpu.make_async_copy(key_hbm, key_ref, weight_sem.at[0])
    value_copy = pltpu.make_async_copy(value_hbm, value_ref, weight_sem.at[1])
    zh, zl = me.z // 2, me.z % 2
    weight_copy = pltpu.make_async_copy(weight_hbm, weight_ref.at[zh], weight_sem.at[2])
    weight_send = pltpu.make_async_remote_copy(
        src_ref=weight_hbm,
        dst_ref=weight_ref.at[zh],
        send_sem=weight_sem.at[3],
        recv_sem=weight_sem.at[4],
        device_id=me.at(z=(me.z + 2) % 4),
        device_id_type=MESH,
    )
    owner = owner_ref[0]
    owner_digit = {"x": owner // 8, "y": (owner // 2) % 4, "z": owner % 2}

    barrier = pltpu.get_barrier_semaphore()
    peers = [me.at(**{a: (getattr(me, a) + d) % 4}) for a in "xyz" for d in (1, 2, 3)]
    peers += [me.at(z=(me.z + d) % 4, c=1 - me.c) for d in range(4)]
    for peer in peers:
        pl.semaphore_signal(barrier, inc=1, device_id=peer, device_id_type=MESH)
    pl.semaphore_wait(barrier, len(peers))

    def own_digit(axis):
        return zh if axis == "z" else getattr(me, axis)

    def source(region, digit):
        lane, kind, unit, tile, base = REGIONS[region]
        view = views[region]
        if kind == "R":
            start = pl.multiple_of(4096 * digit + 2048 * zl, 128)
            return view.at[pl.ds(pl.multiple_of(32 * me.c, 32), 32), pl.ds(start, 2048)]
        cols = pl.ds(tile * 128, 128)
        if lane == 2:
            return view.at[me.c, digit, zl, :, :, :, cols]
        lead = (lane,) if kind == "B" else ()
        if lane == 0:
            return view.at[lead + (me.c * 4 + digit, slice(None), slice(None), zl, slice(None), cols)]
        return view.at[lead + (me.c * 4 + digit, slice(None), zl, slice(None), slice(None), cols)]

    def part(region, step, digit):
        if step == 0:
            return source(region, digit)
        held = landings[region * 3 + step - 1][1]
        lane, kind, unit, tile, base = REGIONS[region]
        if kind == "R":
            width = landings[region * 3 + step][0].shape[2]
            return held.at[:, pl.ds(pl.multiple_of(digit * width, 128), width)]
        return held.at[digit]

    def scatter_copies(region, step):
        axis = ORDERS[REGIONS[region][0]][step]
        slots = landings[region * 3 + step][0]
        index = region * 3 + step
        mine = own_digit(axis)
        copies = []
        own = pltpu.make_async_copy(part(region, step, mine), slots.at[mine], sc_own.at[index])
        for d in (1, 2, 3) if axis != "z" else (2,):
            if axis == "z":
                target, digit = (me.z + 2) % 4, 1 - zh
            else:
                target = digit = (mine + d) % 4
            copies.append(
                pltpu.make_async_remote_copy(
                    src_ref=part(region, step, digit),
                    dst_ref=slots.at[mine],
                    send_sem=sc_send.at[index, d - 1],
                    recv_sem=sc_recv.at[index, d - 1],
                    device_id=me.at(**{axis: target}),
                    device_id_type=MESH,
                )
            )
        return own, copies

    def block(region, level, digits):
        lane, kind, unit, tile, base = REGIONS[region]
        count = unit * 4 ** (3 - level)
        place = 0
        for k in range(3):
            place = place * 4 + (digits[k] if k < level else 0)
        if kind == "R":
            start = pl.multiple_of(128 * place, 128)
            return rot_ref.at[pl.ds(pl.multiple_of(32 * me.c, 32), 32), pl.ds(start, count)]
        start = pl.multiple_of(base + unit * (64 * me.c + place), 32)
        return lat_ref.at[pl.ds(start, count), pl.ds(tile * 128, 128)]

    order = [ORDERS[r[0]] for r in REGIONS]
    digits = [tuple(getattr(me, a) for a in o) for o in order]
    pending = []
    started = []
    for region in range(6):
        own, copies = scatter_copies(region, 0)
        for copy in copies:
            copy.start()
        own.start()
        started.append((own, copies))
    key_copy.start()
    value_copy.start()
    weight_copy.start()
    key_copy.wait()
    latent_queries(q_ref, key_ref, qlat_ref)
    new_keys(q_ref, new_ref, qlat_ref, acc_ref, max_ref, sum_ref)
    for step in range(3):
        following = []
        for region in range(6):
            own, copies = started[region]
            own.wait()
            for copy in copies:
                copy.wait_recv()
            pending += copies
            axis = order[region][step]
            slots, held = landings[region * 3 + step]
            chosen = slots[owner_digit[axis]]
            if step < 2:
                held[...] = chosen
                own, copies = scatter_copies(region, step + 1)
                for copy in copies:
                    copy.start()
                own.start()
                following.append((own, copies))
            else:
                home = block(region, 3, digits[region])
                home[...] = chosen
                following.append(gather_start(region, 3, order, digits, me, block, ag_send, ag_recv))
        started = following

    swaps = []

    def swap(region, which, first):
        ref = block(region, 1, (first, 0, 0))
        copy = pltpu.make_async_remote_copy(
            src_ref=ref,
            dst_ref=ref,
            send_sem=sw_send.at[region, which],
            recv_sem=sw_recv.at[region, which],
            device_id=me.at(c=1 - me.c),
            device_id_type=MESH,
        )
        copy.start()
        swaps.append(copy)

    for level in (3, 2):
        following = []
        for region in range(6):
            for copy in started[region]:
                copy.wait_recv()
            pending += started[region]
            following.append(gather_start(region, level - 1, order, digits, me, block, ag_send, ag_recv))
            if level == 2:
                swap(region, 0, digits[region][0])
        started = following
    for d in (1, 2, 3):
        for region in range(6):
            started[region][d - 1].wait_recv()
            swap(region, d, (digits[region][0] + 4 - d) % 4)
    for region in range(6):
        pending += started[region]
    for copy in swaps:
        copy.wait_recv()
    pending += swaps

    weight_send.start()

    def exchange(chunk):
        for step in range(2):
            copies = []
            for lane, (low, high) in enumerate(EX_LANES):
                axis = EX_ORDERS[lane][step]
                done = EX_ORDERS[lane][:step]
                cols = pl.ds(chunk * CHUNK + low, high - low)
                where = tuple(slice(None) if a in done else getattr(me, a) for a in "xy")
                ref = att_ref.at[where + (slice(None), cols)]
                for d in (1, 2, 3):
                    copy = pltpu.make_async_remote_copy(
                        src_ref=ref,
                        dst_ref=ref,
                        send_sem=ex_send.at[chunk, lane * 2 + step, d - 1],
                        recv_sem=ex_recv.at[chunk, lane * 2 + step, d - 1],
                        device_id=me.at(**{axis: (getattr(me, axis) + d) % 4}),
                        device_id_type=MESH,
                    )
                    copy.start()
                    copies.append(copy)
            yield
            for copy in copies:
                copy.wait_recv()
            pending.extend(copies)

    def partial_out(chunk, half):
        cols = pl.ds(chunk * CHUNK, CHUNK)
        values = att_ref[:, :, :, cols].reshape(512, CHUNK)
        return dot_last(values, weight_ref[half, :, cols])

    active = []
    for chunk in range(CHUNKS):
        for piece in range(2):
            prefix_keys(chunk * ROWS, piece * 4, 4, q_ref, qlat_ref, lat_ref, rot_ref, score_ref, acc_ref, max_ref, sum_ref)
            if active and piece == 0:
                next(active[-1])
        if chunk == 0:
            value_copy.wait()
        attended_values(chunk, acc_ref, sum_ref, value_ref, att_ref, (me.x, me.y))
        active.append(exchange(chunk))
        next(active[-1])
    weight_copy.wait()
    for chunk in range(CHUNKS - 1):
        for _ in active[chunk]:
            pass
        if chunk == 0:
            next(active[-1])
            weight_send.wait_recv()

        @pl.loop(0, 2)
        def _(half):
            term = partial_out(chunk, half)
            total_ref[half] = term if chunk == 0 else total_ref[half] + term
    for _ in active[-1]:
        pass
    sends = []
    for far in (1, 0):
        half = 1 - zh if far else zh
        total_ref[half] = total_ref[half] + partial_out(CHUNKS - 1, half)
        for flip_z in (1, 0):
            for flip_c in (1, 0):
                target_l = 1 - zl if flip_z else zl
                target_c = 1 - me.c if flip_c else me.c
                slot = 4 * far + 2 * flip_z + flip_c
                if slot == 0:
                    continue
                rows = pl.ds(pl.multiple_of((target_l * 2 + target_c) * 128, 128), 128)
                part_ref[slot] = total_ref[half, rows, :].astype(BF)
                copy = pltpu.make_async_remote_copy(
                    src_ref=part_ref.at[slot],
                    dst_ref=land_ref.at[slot],
                    send_sem=rs_send.at[slot],
                    recv_sem=rs_recv.at[slot],
                    device_id=me.at(z=half * 2 + target_l, c=target_c),
                    device_id_type=MESH,
                )
                copy.start()
                sends.append(copy)
    for copy in sends:
        copy.wait_recv()
    own_rows = pl.ds(pl.multiple_of((zl * 2 + me.c) * 128, 128), 128)
    for far in (0, 1):
        result = land_ref[4 * far + 1].astype(jnp.float32) + land_ref[4 * far + 2].astype(jnp.float32)
        result = result + land_ref[4 * far + 3].astype(jnp.float32)
        result = result + (land_ref[4].astype(jnp.float32) if far else total_ref[zh, own_rows, :])
        out_ref[:, 1 - zh if far else zh] = result.astype(BF).reshape(4, 32, 224)
    weight_send.wait_send()
    for copy in pending + sends:
        copy.wait_send()


CHUNKS = 4
CHUNK = 4096 // CHUNKS
EX_ORDERS = (("x", "y"), ("y", "x"))
EX_LANES = ((0, CHUNK // 2), (CHUNK // 2, CHUNK))
SCALE = 192**-0.5 * 1.4426950408889634
LAST = (((1,), (1,)), ((), ()))
ROWS = 1024 // CHUNKS
KEYS = 1024


def dot(a, b):
    return jnp.dot(a, b, preferred_element_type=jnp.float32)


def dot_last(a, b):
    return lax.dot_general(a, b, LAST, preferred_element_type=jnp.float32)


def latent_queries(q_ref, key_ref, qlat_ref):
    @pl.loop(0, 32, unroll=4)
    def _(h):
        rows = pl.ds(pl.multiple_of(h * 32, 32), 32)
        qlat_ref[rows, :] = dot(q_ref[rows, 0:128], key_ref[h]).astype(BF)


def new_keys(q_ref, new_ref, qlat_ref, acc_ref, max_ref, sum_ref):
    @pl.loop(0, 1024 // ROWS)
    def _(r):
        rows = pl.ds(pl.multiple_of(r * ROWS, ROWS), ROWS)
        scores = dot_last(qlat_ref[rows, :], new_ref[:, 0:512])
        scores = (scores + dot_last(q_ref[rows, 128:192], new_ref[:, 512:576])) * SCALE
        row = lax.broadcasted_iota(jnp.int32, (ROWS, 32), 0) % 32
        key = lax.broadcasted_iota(jnp.int32, (ROWS, 32), 1)
        visible = (row // 4 == key // 4) & (key <= row)
        top = jnp.max(jnp.where(visible, scores, -jnp.inf), axis=1, keepdims=True)
        e = jnp.where(visible, jnp.exp2(jnp.where(visible, scores, top) - top), 0.0)
        max_ref[rows, :] = jnp.broadcast_to(top, (ROWS, 128))
        sum_ref[rows, :] = jnp.broadcast_to(jnp.sum(e, axis=1, keepdims=True), (ROWS, 128))
        acc_ref[rows, :] = dot(e.astype(BF), new_ref[:, 0:512])


def prefix_keys(row, first, count, q_ref, qlat_ref, lat_ref, rot_ref, score_ref, acc_ref, max_ref, sum_ref):
    rows = pl.ds(row, ROWS)

    def scores(k):
        keys = pl.ds(pl.multiple_of(k * KEYS, KEYS), KEYS)
        return dot_last(qlat_ref[rows, :], lat_ref[keys, :]) + dot(q_ref[rows, 128:192], rot_ref[:, keys])

    def take(k, s):
        keys = pl.ds(pl.multiple_of(k * KEYS, KEYS), KEYS)
        old = max_ref[rows, :]
        new = jnp.maximum(old, jnp.max(s, axis=1, keepdims=True) * SCALE)
        max_ref[rows, :] = new
        shrink = jnp.exp2(old - new)
        e = jnp.exp2(s * SCALE - new[:, 0:1])
        sum_ref[rows, :] = sum_ref[rows, :] * shrink + jnp.sum(e, axis=1, keepdims=True)
        acc_ref[rows, :] = acc_ref[rows, :] * shrink[:, 0:1] + dot(e.astype(BF), lat_ref[keys, :])

    if first == 0:
        score_ref[0] = scores(0)

    @pl.loop(first // 2, (first + count) // 2)
    def _(pair):
        k = pair * 2
        s = score_ref[0]
        score_ref[1] = scores(k + 1)
        take(k, s)
        s = score_ref[1]
        score_ref[0] = scores(jnp.minimum(k + 2, 8192 // KEYS - 1))
        take(k + 1, s)


def attended_values(chunk, acc_ref, sum_ref, value_ref, att_ref, place):
    heads = 32 // CHUNKS

    @pl.loop(chunk * heads, (chunk + 1) * heads, unroll=4)
    def _(h):
        rows = pl.ds(pl.multiple_of(h * 32, 32), 32)
        context = (acc_ref[rows, :] / sum_ref[rows, 0:1]).astype(BF)
        cols = pl.ds(pl.multiple_of(h * 128, 128), 128)
        att_ref[place + (slice(None), cols)] = dot(context, value_ref[h]).astype(BF)


def gather_start(region, level, order, digits, me, block, ag_send, ag_recv):
    axis = order[region][level - 1]
    ref = block(region, level, digits[region])
    copies = []
    for d in (1, 2, 3):
        copy = pltpu.make_async_remote_copy(
            src_ref=ref,
            dst_ref=ref,
            send_sem=ag_send.at[region, level - 1, d - 1],
            recv_sem=ag_recv.at[region, level - 1, d - 1],
            device_id=me.at(**{axis: (getattr(me, axis) + d) % 4}),
            device_id_type=MESH,
        )
        copy.start()
        copies.append(copy)
    return copies


def layer(owner_index, queries, new_kv, key_up, value_up, out_weight, latent, rope):
    sem = pltpu.SemaphoreType.DMA
    f32 = jnp.float32
    scratch = [
        pltpu.VMEM((8192, 512), BF),
        pltpu.VMEM((64, 8192), BF),
        pltpu.VMEM((32, 128, 512), BF),
        pltpu.VMEM((32, 512, 128), BF),
        pltpu.VMEM((2, 224, 4096), BF),
        pltpu.VMEM((1024, 512), BF),
        pltpu.VMEM((2, ROWS, KEYS), f32),
        pltpu.VMEM((1024, 512), f32),
        pltpu.VMEM((1024, 128), f32),
        pltpu.VMEM((1024, 128), f32),
        pltpu.VMEM((4, 4, 32, 4096), BF),
        pltpu.VMEM((2, 512, 224), f32),
        pltpu.VMEM((8, 128, 224), BF),
        pltpu.VMEM((8, 128, 224), BF),
        sem((5,)),
        sem((CHUNKS, 4, 3)),
        sem((CHUNKS, 4, 3)),
        sem((8,)),
        sem((8,)),
    ]
    for slots, held in landing_shapes():
        scratch += [pltpu.VMEM(slots, BF), pltpu.VMEM(held, BF)]
    scratch += [sem((18, 3)), sem((18, 3)), sem((18,)), sem((6, 3, 3)), sem((6, 3, 3)), sem((6, 4)), sem((6, 4))]
    hbm = pl.BlockSpec(memory_space=pl.ANY)
    vmem = pl.BlockSpec(memory_space=pltpu.VMEM)
    return pl.pallas_call(
        layer_kernel,
        out_shape=jax.ShapeDtypeStruct((4, 2, 32, 224), BF),
        in_specs=[pl.BlockSpec(memory_space=pltpu.SMEM), vmem, vmem] + [hbm] * 9,
        out_specs=vmem,
        scratch_shapes=scratch,
        compiler_params=pltpu.CompilerParams(
            collective_id=0, has_side_effects=True, vmem_limit_bytes=60 << 20
        ),
        name="layer",
    )(owner_index, queries, new_kv, key_up, value_up, out_weight, *source_views(latent), rope)


def body(queries, new_kv, owner_index, prefix_latent, prefix_rope, key_up, value_up, out_weight):
    samples, steps, heads, width = queries.shape
    rows = jnp.transpose(queries.reshape(samples * steps, heads, width), (1, 0, 2)).reshape(-1, width)
    out = layer(
        owner_index, rows, new_kv.reshape(samples * steps, -1), key_up, value_up, out_weight.T, prefix_latent[0], prefix_rope[0]
    )
    return out.reshape(64, steps, -1)


def solution(mesh):
    return jax.shard_map(
        body,
        mesh=mesh,
        in_specs=(
            P("grp", None, "tp", None),
            P("grp", None, None),
            P(),
            P("grp", None, None),
            P("grp", None, None),
            P("tp", None, None),
            P("tp", None, None),
            P("tp", "grp"),
        ),
        out_specs=P("tp", None, "grp"),
        check_vma=False,
    )
```

```python
import functools
import jax
import jax.numpy as jnp
from jax import lax
from jax.experimental import pallas as pl
from jax.experimental.pallas import tpu as pltpu
from jax.sharding import PartitionSpec as P

MESH = pl.DeviceIdType.MESH
BF = jnp.bfloat16


class Coord:
    def __init__(self):
        g, t = lax.axis_index("grp"), lax.axis_index("tp")
        self.x, self.y, self.z, self.c = g // 8, (g // 2) % 4, (g % 2) * 2 + t // 2, t % 2

    def at(self, **moved):
        x, y, z, c = (moved.get(k, getattr(self, k)) for k in "xyzc")
        return (x * 8 + y * 2 + z // 2, (z % 2) * 2 + c)


ORDERS = (("x", "y", "z"), ("y", "z", "x"), ("z", "x", "y"))
REGIONS = (
    (0, "A", 32, 0, 0),
    (0, "B", 16, 3, 0),
    (1, "A", 32, 1, 0),
    (1, "B", 16, 3, 2048),
    (2, "A", 32, 2, 0),
    (2, "R", 128, None, None),
)


def source_views(latent):
    return (
        latent.reshape(2, 8, 4, 2, 2, 32, 512),
        latent.reshape(2, 2, 8, 4, 2, 2, 16, 512),
        latent.reshape(2, 8, 2, 2, 4, 32, 512),
        latent.reshape(2, 2, 8, 2, 2, 4, 16, 512),
        latent.reshape(2, 2, 2, 2, 4, 4, 32, 512),
    )


def landing_shapes():
    shapes = []
    for lane, kind, unit, _, _ in REGIONS:
        dims = ((4, 4, 2), (4, 2, 4), (2, 4, 4))[lane]
        for step in range(3):
            if kind == "R":
                width = unit
                for d in dims[step + 1 :]:
                    width *= d
                shapes.append(((dims[step], 16, width), (16, width)))
            else:
                tail = dims[step + 1 :] + (unit, 128)
                shapes.append(((dims[step],) + tail, tail))
    return shapes


def layer_kernel(
    owner_ref, q_ref, new_ref, key_hbm, value_hbm, weight_hbm, v0, v1, v2, v3, v4, rope_ref, out_ref,
    lat_ref, rot_ref, key_ref, value_ref, weight_ref, qlat_ref, acc_ref, max_ref, sum_ref,
    att_ref, total_ref, part_ref, land_ref, weight_sem, ex_send, ex_recv, rs_send, rs_recv, *scratch
):
    me = Coord()
    views = (v0, v1, v2, v3, v4, rope_ref)
    landings = [(scratch[2 * i], scratch[2 * i + 1]) for i in range(36)]
    sc_send, sc_recv, sc_own, ag_send, ag_recv, sw_send, sw_recv = scratch[72:]
    key_copy = pltpu.make_async_copy(key_hbm, key_ref, weight_sem.at[0])
    value_copy = pltpu.make_async_copy(value_hbm, value_ref, weight_sem.at[1])
    zh, zl = me.z // 2, me.z % 2
    weight_copy = pltpu.make_async_copy(weight_hbm, weight_ref.at[zh], weight_sem.at[2])
    weight_sends = [
        pltpu.make_async_remote_copy(
            src_ref=weight_hbm.at[:, pl.ds(i * CHUNK, CHUNK)],
            dst_ref=weight_ref.at[zh, :, pl.ds(i * CHUNK, CHUNK)],
            send_sem=weight_sem.at[3 + i],
            recv_sem=weight_sem.at[3 + CHUNKS + i],
            device_id=me.at(z=(me.z + 2) % 4),
            device_id_type=MESH,
        )
        for i in range(CHUNKS)
    ]
    owner = owner_ref[0]
    owner_digit = {"x": owner // 8, "y": (owner // 2) % 4, "z": owner % 2}

    barrier = pltpu.get_barrier_semaphore()
    peers = [me.at(**{a: (getattr(me, a) + d) % 4}) for a in "xyz" for d in (1, 2, 3)]
    peers += [me.at(z=(me.z + d) % 4, c=1 - me.c) for d in range(4)]
    for peer in peers:
        pl.semaphore_signal(barrier, inc=1, device_id=peer, device_id_type=MESH)
    pl.semaphore_wait(barrier, len(peers))

    def own_digit(axis):
        return zh if axis == "z" else getattr(me, axis)

    rope_rows = pl.ds(pl.multiple_of(32 * me.c + 16 * zl, 16), 16)

    def source(h, region, digit):
        lane, kind, unit, tile, base = REGIONS[region]
        view = views[region]
        if kind == "R":
            return view.at[rope_rows, pl.ds(pl.multiple_of(4096 * h + 2048 * digit, 128), 2048)]
        cols = pl.ds(tile * 128, 128)
        if lane == 2:
            return view.at[h, me.c, digit, zl, :, :, :, cols]
        lead = (h, lane) if kind == "B" else (h,)
        if lane == 0:
            return view.at[lead + (me.c * 4 + digit, slice(None), slice(None), zl, slice(None), cols)]
        return view.at[lead + (me.c * 4 + digit, slice(None), zl, slice(None), slice(None), cols)]

    def part(h, region, step, digit):
        if step == 0:
            return source(h, region, digit)
        held = landings[h * 18 + region * 3 + step - 1][1]
        if REGIONS[region][1] == "R":
            width = landings[h * 18 + region * 3 + step][0].shape[2]
            return held.at[:, pl.ds(pl.multiple_of(digit * width, 128), width)]
        return held.at[digit]

    def scatter_copies(h, region, step):
        axis = ORDERS[REGIONS[region][0]][step]
        index = h * 18 + region * 3 + step
        slots = landings[index][0]
        mine = own_digit(axis)
        copies = []
        own = pltpu.make_async_copy(part(h, region, step, mine), slots.at[mine], sc_own.at[index])
        for d in (1, 2, 3) if axis != "z" else (2,):
            if axis == "z":
                target, digit = (me.z + 2) % 4, 1 - zh
            else:
                target = digit = (mine + d) % 4
            copies.append(
                pltpu.make_async_remote_copy(
                    src_ref=part(h, region, step, digit),
                    dst_ref=slots.at[mine],
                    send_sem=sc_send.at[index, d - 1],
                    recv_sem=sc_recv.at[index, d - 1],
                    device_id=me.at(**{axis: target}),
                    device_id_type=MESH,
                )
            )
        return own, copies

    def block(h, region, level, digits):
        lane, kind, unit, tile, base = REGIONS[region]
        count = unit * 4 ** (3 - level)
        place = 0
        for i in range(3):
            place = place * 4 + (digits[i] if i < level else 0)
        if kind == "R":
            place = place - digits[0] * 16 + (digits[0] // 2) * 16
            rows = pl.ds(pl.multiple_of(32 * me.c + 16 * (digits[0] % 2), 16), 16)
            return rot_ref.at[rows, pl.ds(pl.multiple_of(4096 * h + 128 * place, 128), count)]
        start = pl.multiple_of(4096 * h + base + unit * (64 * me.c + place), 16)
        return lat_ref.at[pl.ds(start, count), pl.ds(tile * 128, 128)]

    order = [ORDERS[r[0]] for r in REGIONS]
    digits = [tuple(getattr(me, a) for a in o) for o in order]
    pending = []

    def gather_start(h, region, level):
        axis = order[region][level - 1]
        ref = block(h, region, level, digits[region])
        copies = []
        for d in (1, 2, 3):
            copy = pltpu.make_async_remote_copy(
                src_ref=ref,
                dst_ref=ref,
                send_sem=ag_send.at[h * 6 + region, level - 1, d - 1],
                recv_sem=ag_recv.at[h * 6 + region, level - 1, d - 1],
                device_id=me.at(**{axis: (getattr(me, axis) + d) % 4}),
                device_id_type=MESH,
            )
            copy.start()
            copies.append(copy)
        return copies

    def prefix_half(h):
        started = []
        for region in range(6):
            own, copies = scatter_copies(h, region, 0)
            for copy in copies:
                copy.start()
            own.start()
            started.append((own, copies))
        for step in range(3):
            yield
            following = []
            for region in range(6):
                own, copies = started[region]
                own.wait()
                for copy in copies:
                    copy.wait_recv()
                pending.extend(copies)
                slots, held = landings[h * 18 + region * 3 + step]
                chosen = slots[owner_digit[order[region][step]]]
                if step < 2:
                    held[...] = chosen
                    own, copies = scatter_copies(h, region, step + 1)
                    for copy in copies:
                        copy.start()
                    own.start()
                    following.append((own, copies))
                else:
                    home = block(h, region, 3, digits[region])
                    home[...] = chosen
                    following.append(gather_start(h, region, 3))
            started = following
        swaps = []

        def swap(region, which, first):
            ref = block(h, region, 1, (first, 0, 0))
            copy = pltpu.make_async_remote_copy(
                src_ref=ref,
                dst_ref=ref,
                send_sem=sw_send.at[h * 6 + region, which],
                recv_sem=sw_recv.at[h * 6 + region, which],
                device_id=me.at(c=1 - me.c),
                device_id_type=MESH,
            )
            copy.start()
            swaps.append(copy)

        for level in (3, 2):
            yield
            following = []
            for region in range(6):
                for copy in started[region]:
                    copy.wait_recv()
                pending.extend(started[region])
                following.append(gather_start(h, region, level - 1))
            if level == 2:
                for region in range(6):
                    swap(region, 0, digits[region][0])
            started = following
        yield
        for d in (1, 3, 2):
            for region in range(6):
                started[region][d - 1].wait_recv()
                swap(region, d, (digits[region][0] + 4 - d) % 4)
        for region in range(6):
            pending.extend(started[region])
        yield
        for copy in swaps:
            copy.wait_recv()
        pending.extend(swaps)

    first, second = prefix_half(0), prefix_half(1)
    next(first)
    key_copy.start()
    value_copy.start()
    weight_copy.start()
    key_copy.wait()
    latent_queries(0, 8, q_ref, key_ref, qlat_ref)
    next(first)
    next(second)
    latent_queries(8, 16, q_ref, key_ref, qlat_ref)
    next(first)
    latent_queries(16, 24, q_ref, key_ref, qlat_ref)
    next(first)
    latent_queries(24, 32, q_ref, key_ref, qlat_ref)
    next(first)
    next(second)
    new_keys(q_ref, new_ref, qlat_ref, acc_ref, max_ref, sum_ref)
    next(first)
    next(second)
    next(second)
    next(second)
    next(first)
    next(second)
    for _ in first:
        pass
    all_rows(0, 2, q_ref, qlat_ref, lat_ref, rot_ref, acc_ref, max_ref, sum_ref)
    weight_sends[0].start()
    all_rows(2, 3, q_ref, qlat_ref, lat_ref, rot_ref, acc_ref, max_ref, sum_ref)
    next(second)
    all_rows(3, 4, q_ref, qlat_ref, lat_ref, rot_ref, acc_ref, max_ref, sum_ref)
    for copy in weight_sends[1:]:
        copy.start()
    for _ in second:
        pass

    def exchange(chunk):
        for step in range(2):
            copies = []
            for lane, (low, high) in enumerate(EX_LANES):
                axis = EX_ORDERS[lane][step]
                done = EX_ORDERS[lane][:step]
                cols = pl.ds(chunk * CHUNK + low, high - low)
                where = tuple(slice(None) if a in done else getattr(me, a) for a in "xy")
                ref = att_ref.at[where + (slice(None), cols)]
                for d in (1, 2, 3):
                    copy = pltpu.make_async_remote_copy(
                        src_ref=ref,
                        dst_ref=ref,
                        send_sem=ex_send.at[chunk, lane * 2 + step, d - 1],
                        recv_sem=ex_recv.at[chunk, lane * 2 + step, d - 1],
                        device_id=me.at(**{axis: (getattr(me, axis) + d) % 4}),
                        device_id_type=MESH,
                    )
                    copy.start()
                    copies.append(copy)
            yield
            for copy in copies:
                copy.wait_recv()
            pending.extend(copies)

    def partial_out(chunk, half):
        cols = pl.ds(chunk * CHUNK, CHUNK)
        values = att_ref[:, :, :, cols].reshape(512, CHUNK)
        return dot_last(values, weight_ref[half, :, cols])

    active = []
    for chunk in range(CHUNKS):
        chunk_rows(chunk * ROWS, 4, 8, q_ref, qlat_ref, lat_ref, rot_ref, acc_ref, max_ref, sum_ref)
        if active:
            next(active[-1])
        if chunk == 0:
            value_copy.wait()
        attended_values(chunk, acc_ref, sum_ref, value_ref, att_ref, (me.x, me.y))
        active.append(exchange(chunk))
        next(active[-1])
    weight_copy.wait()
    for chunk in range(CHUNKS - 1):
        for _ in active[chunk]:
            pass
        if chunk == 0:
            next(active[-1])

        weight_sends[chunk].wait_recv()

        @pl.loop(0, 2)
        def _(half):
            term = partial_out(chunk, half)
            total_ref[half] = term if chunk == 0 else total_ref[half] + term
    for _ in active[-1]:
        pass
    weight_sends[-1].wait_recv()
    sends = []
    for far in (1, 0):
        half = 1 - zh if far else zh
        total_ref[half] = total_ref[half] + partial_out(CHUNKS - 1, half)
        for flip_z in (1, 0):
            for flip_c in (1, 0):
                target_l = 1 - zl if flip_z else zl
                target_c = 1 - me.c if flip_c else me.c
                slot = 4 * far + 2 * flip_z + flip_c
                if slot == 0:
                    continue
                rows = pl.ds(pl.multiple_of((target_l * 2 + target_c) * 128, 128), 128)
                part_ref[slot] = total_ref[half, rows, :].astype(BF)
                copy = pltpu.make_async_remote_copy(
                    src_ref=part_ref.at[slot],
                    dst_ref=land_ref.at[slot],
                    send_sem=rs_send.at[slot],
                    recv_sem=rs_recv.at[slot],
                    device_id=me.at(z=half * 2 + target_l, c=target_c),
                    device_id_type=MESH,
                )
                copy.start()
                sends.append(copy)
    for copy in sends:
        copy.wait_recv()
    own_rows = pl.ds(pl.multiple_of((zl * 2 + me.c) * 128, 128), 128)
    for far in (0, 1):
        result = land_ref[4 * far + 1].astype(jnp.float32) + land_ref[4 * far + 2].astype(jnp.float32)
        result = result + land_ref[4 * far + 3].astype(jnp.float32)
        result = result + (land_ref[4].astype(jnp.float32) if far else total_ref[zh, own_rows, :])
        out_ref[:, 1 - zh if far else zh] = result.astype(BF).reshape(4, 32, 224)
    for copy in pending + sends + weight_sends:
        copy.wait_send()


CHUNKS = 4
CHUNK = 4096 // CHUNKS
EX_ORDERS = (("x", "y"), ("y", "x"))
EX_LANES = ((0, CHUNK // 2), (CHUNK // 2, CHUNK))
SCALE = 192**-0.5 * 1.4426950408889634
LAST = (((1,), (1,)), ((), ()))
ROWS = 1024 // CHUNKS
KEYS = 1024


def dot(a, b):
    return jnp.dot(a, b, preferred_element_type=jnp.float32)


def dot_last(a, b):
    return lax.dot_general(a, b, LAST, preferred_element_type=jnp.float32)


def latent_queries(low, high, q_ref, key_ref, qlat_ref):
    @pl.loop(low, high, unroll=4)
    def _(h):
        rows = pl.ds(pl.multiple_of(h * 32, 32), 32)
        qlat_ref[rows, :] = dot(q_ref[rows, 0:128], key_ref[h]).astype(BF)


def new_keys(q_ref, new_ref, qlat_ref, acc_ref, max_ref, sum_ref):
    @pl.loop(0, 4)
    def _(r):
        rows = pl.ds(pl.multiple_of(r * ROWS, ROWS), ROWS)
        scores = dot_last(qlat_ref[rows, :], new_ref[:, 0:512])
        scores = (scores + dot_last(q_ref[rows, 128:192], new_ref[:, 512:576])) * SCALE
        row = lax.broadcasted_iota(jnp.int32, (ROWS, 32), 0) % 32
        key = lax.broadcasted_iota(jnp.int32, (ROWS, 32), 1)
        visible = (row // 4 == key // 4) & (key <= row)
        top = jnp.max(jnp.where(visible, scores, -jnp.inf), axis=1, keepdims=True)
        e = jnp.where(visible, jnp.exp2(jnp.where(visible, scores, top) - top), 0.0)
        max_ref[rows, :] = jnp.broadcast_to(top, (ROWS, 128))
        sum_ref[rows, :] = jnp.broadcast_to(jnp.sum(e, axis=1, keepdims=True), (ROWS, 128))
        acc_ref[rows, :] = dot(e.astype(BF), new_ref[:, 0:512])


def block_scores(rows, k, q_ref, qlat_ref, lat_ref, rot_ref):
    keys = pl.ds(pl.multiple_of(k * KEYS, KEYS), KEYS)
    return dot_last(qlat_ref[rows, :], lat_ref[keys, :]) + dot(q_ref[rows, 128:192], rot_ref[:, keys])


def take(rows, k, s, lat_ref, acc_ref, max_ref, sum_ref):
    keys = pl.ds(pl.multiple_of(k * KEYS, KEYS), KEYS)
    old = max_ref[rows, :]
    new = jnp.maximum(old, jnp.max(s, axis=1, keepdims=True) * SCALE)
    max_ref[rows, :] = new
    shrink = jnp.exp2(old - new)
    e = jnp.exp2(s * SCALE - new[:, 0:1])
    sum_ref[rows, :] = sum_ref[rows, :] * shrink + jnp.sum(e, axis=1, keepdims=True)
    acc_ref[rows, :] = acc_ref[rows, :] * shrink[:, 0:1] + dot(e.astype(BF), lat_ref[keys, :])


def all_rows(low, high, q_ref, qlat_ref, lat_ref, rot_ref, acc_ref, max_ref, sum_ref):
    @pl.loop(low, high)
    def _(k):
        halves = [pl.ds(0, 512), pl.ds(512, 512)]
        scores = [block_scores(rows, k, q_ref, qlat_ref, lat_ref, rot_ref) for rows in halves]
        for rows, s in zip(halves, scores):
            take(rows, k, s, lat_ref, acc_ref, max_ref, sum_ref)


def chunk_rows(row, low, high, q_ref, qlat_ref, lat_ref, rot_ref, acc_ref, max_ref, sum_ref):
    rows = pl.ds(row, ROWS)
    s = block_scores(rows, low, q_ref, qlat_ref, lat_ref, rot_ref)
    for k in range(low, high):
        following = block_scores(rows, k + 1, q_ref, qlat_ref, lat_ref, rot_ref) if k + 1 < high else None
        take(rows, k, s, lat_ref, acc_ref, max_ref, sum_ref)
        s = following


def attended_values(chunk, acc_ref, sum_ref, value_ref, att_ref, place):
    heads = 32 // CHUNKS

    @pl.loop(chunk * heads, (chunk + 1) * heads, unroll=4)
    def _(h):
        rows = pl.ds(pl.multiple_of(h * 32, 32), 32)
        context = (acc_ref[rows, :] / sum_ref[rows, 0:1]).astype(BF)
        cols = pl.ds(pl.multiple_of(h * 128, 128), 128)
        att_ref[place + (slice(None), cols)] = dot(context, value_ref[h]).astype(BF)


def layer(owner_index, queries, new_kv, key_up, value_up, out_weight, latent, rope):
    sem = pltpu.SemaphoreType.DMA
    f32 = jnp.float32
    scratch = [
        pltpu.VMEM((8192, 512), BF),
        pltpu.VMEM((64, 8192), BF),
        pltpu.VMEM((32, 128, 512), BF),
        pltpu.VMEM((32, 512, 128), BF),
        pltpu.VMEM((2, 224, 4096), BF),
        pltpu.VMEM((1024, 512), BF),
        pltpu.VMEM((1024, 512), f32),
        pltpu.VMEM((1024, 128), f32),
        pltpu.VMEM((1024, 128), f32),
        pltpu.VMEM((4, 4, 32, 4096), BF),
        pltpu.VMEM((2, 512, 224), f32),
        pltpu.VMEM((8, 128, 224), BF),
        pltpu.VMEM((8, 128, 224), BF),
        sem((3 + 2 * CHUNKS,)),
        sem((CHUNKS, 4, 3)),
        sem((CHUNKS, 4, 3)),
        sem((8,)),
        sem((8,)),
    ]
    for slots, held in landing_shapes() * 2:
        scratch += [pltpu.VMEM(slots, BF), pltpu.VMEM(held, BF)]
    scratch += [sem((36, 3)), sem((36, 3)), sem((36,)), sem((12, 3, 3)), sem((12, 3, 3)), sem((12, 4)), sem((12, 4))]
    hbm = pl.BlockSpec(memory_space=pl.ANY)
    vmem = pl.BlockSpec(memory_space=pltpu.VMEM)
    return pl.pallas_call(
        layer_kernel,
        out_shape=jax.ShapeDtypeStruct((4, 2, 32, 224), BF),
        in_specs=[pl.BlockSpec(memory_space=pltpu.SMEM), vmem, vmem] + [hbm] * 9,
        out_specs=vmem,
        scratch_shapes=scratch,
        compiler_params=pltpu.CompilerParams(
            collective_id=0, has_side_effects=True, vmem_limit_bytes=60 << 20
        ),
        name="layer",
    )(owner_index, queries, new_kv, key_up, value_up, out_weight, *source_views(latent), rope)


def body(queries, new_kv, owner_index, prefix_latent, prefix_rope, key_up, value_up, out_weight):
    samples, steps, heads, width = queries.shape
    rows = jnp.transpose(queries.reshape(samples * steps, heads, width), (1, 0, 2)).reshape(-1, width)
    out = layer(
        owner_index, rows, new_kv.reshape(samples * steps, -1), key_up, value_up, out_weight.T, prefix_latent[0], prefix_rope[0]
    )
    return out.reshape(64, steps, -1)


def solution(mesh):
    return jax.shard_map(
        body,
        mesh=mesh,
        in_specs=(
            P("grp", None, "tp", None),
            P("grp", None, None),
            P(),
            P("grp", None, None),
            P("grp", None, None),
            P("tp", None, None),
            P("tp", None, None),
            P("tp", "grp"),
        ),
        out_specs=P("tp", None, "grp"),
        check_vma=False,
    )
```

```python
import functools
import jax
import jax.numpy as jnp
from jax import lax
from jax.experimental import pallas as pl
from jax.experimental.pallas import tpu as pltpu
from jax.sharding import PartitionSpec as P

MESH = pl.DeviceIdType.MESH
BF = jnp.bfloat16
F32 = jnp.float32
CHUNKS = 4
CHUNK = 4096 // CHUNKS
ROWS = 1024 // CHUNKS


class Coord:
    def __init__(self):
        g, t = lax.axis_index("grp"), lax.axis_index("tp")
        self.x, self.y, self.z, self.c = g // 8, (g // 2) % 4, (g % 2) * 2 + t // 2, t % 2

    def at(self, **moved):
        x, y, z, c = (moved.get(k, getattr(self, k)) for k in "xyzc")
        return (x * 8 + y * 2 + z // 2, (z % 2) * 2 + c)


ORDERS = (("x", "y", "z"), ("y", "z", "x"), ("z", "x", "y"), ("z", "x", "y"))
BASES = (0, 3072, 6144)
SHARE = ((768, 192, 96), (768, 384, 96), (512, 128, 32), (2048, 512, 128))
ROPE = 3


def landing_shapes():
    shapes = []
    for region in range(4):
        for step in range(3):
            share = SHARE[region][step]
            one = (32, share) if region == ROPE else (share, 256 if region == 2 else 128)
            slots = 2 if ORDERS[region][step] == "z" else 4
            shapes.append(((slots,) + one, one))
    return shapes


def wait_bytes(ref, sem):
    pltpu.make_async_copy(ref, ref, sem).wait()


def layer_kernel(
    owner_ref, q_ref, new_ref, key_hbm, value_hbm, weight_hbm, latent_hbm, rope_hbm, out_ref,
    lat_ref, rot_ref, key_ref, value_ref, weight_ref, qlat_ref, acc_ref, max_ref, sum_ref,
    att_ref, total_ref, part_ref, land_ref, local_sem, weight_send, weight_recv, sc_send, sc_recv, sc_own,
    ag_send, ag_recv, last_send, last_recv, sw_send, sw_recv, ex_send, ex_recv, rs_sem, *landings
):
    me = Coord()
    zh, zl = me.z // 2, me.z % 2
    owner = owner_ref[0]
    owner_digit = {"x": owner // 8, "y": (owner // 2) % 4, "z": owner % 2}
    key_copy = pltpu.make_async_copy(key_hbm, key_ref, local_sem.at[0])
    value_copy = pltpu.make_async_copy(value_hbm, value_ref, local_sem.at[1])
    weight_copy = pltpu.make_async_copy(weight_hbm, weight_ref.at[zh], local_sem.at[2])
    drains = []

    def send(src, dst, send_sem, recv_sem, device):
        copy = pltpu.make_async_remote_copy(
            src_ref=src, dst_ref=dst, send_sem=send_sem, recv_sem=recv_sem, device_id=device, device_id_type=MESH
        )
        copy.start()
        return copy

    def beside(axis, d):
        return me.at(**{axis: (getattr(me, axis) + d) % 4})

    barrier = pltpu.get_barrier_semaphore()
    peers = [beside(a, d) for a in "xyz" for d in (1, 2, 3)]
    peers += [me.at(z=(me.z + d) % 4, c=1 - me.c) for d in range(4)]
    peers += [me.at(x=(me.x + i) % 4, y=(me.y + j) % 4) for i in (1, 2, 3) for j in (1, 2, 3)]
    for peer in peers:
        pl.semaphore_signal(barrier, inc=1, device_id=peer, device_id_type=MESH)
    pl.semaphore_wait(barrier, len(peers))

    cols = pl.ds(pl.multiple_of(256 * me.c, 256), 256)
    rope_rows = pl.ds(pl.multiple_of(32 * me.c, 32), 32)

    def own_digit(axis):
        return zh if axis == "z" else getattr(me, axis)

    tile = pl.ds(pl.multiple_of(256 * me.c + 128 * zl, 128), 128)

    def source(region, digit):
        if region == ROPE:
            return rope_hbm.at[rope_rows, pl.ds(pl.multiple_of(4096 * digit + 2048 * zl, 128), 2048)]
        if region == 2:
            return latent_hbm.at[pl.ds(pl.multiple_of(6144 + 1024 * digit + 512 * zl, 512), 512), cols]
        return latent_hbm.at[pl.ds(pl.multiple_of(BASES[region] + 768 * digit, 256), 768), tile]

    def part(region, step, digit):
        if step == 0:
            return source(region, digit)
        held = landings[2 * (region * 3 + step - 1) + 1]
        share = SHARE[region][step]
        if region == ROPE:
            return held.at[:, pl.ds(pl.multiple_of(digit * share, 128), share)]
        return held.at[pl.ds(pl.multiple_of(digit * share, 32), share)]

    def scatter(region, step):
        axis = ORDERS[region][step]
        index = region * 3 + step
        slots = landings[2 * index]
        mine = own_digit(axis)
        if axis == "z":
            send(part(region, step, 1 - zh), slots.at[mine], sc_send.at[index], sc_recv.at[index], beside("z", 2))
        else:
            for d in (1, 3, 2):
                digit = (mine + d) % 4
                send(part(region, step, digit), slots.at[mine], sc_send.at[index], sc_recv.at[index], beside(axis, d))
        pltpu.make_async_copy(part(region, step, mine), slots.at[mine], sc_own.at[index]).start()
        others = slots.at[pl.ds(0, slots.shape[0] - 1)]
        drains.append((others, sc_send.at[index]))

    def pick(region, step):
        index = region * 3 + step
        slots = landings[2 * index]
        wait_bytes(slots.at[0], sc_own.at[index])
        wait_bytes(slots.at[pl.ds(0, slots.shape[0] - 1)], sc_recv.at[index])
        return slots[owner_digit[ORDERS[region][step]]]

    def extent(region, level):
        if region in (0, 1):
            return (768, (192, 384)[region], 96)[level - 1], level == 3 or (region, level) == (1, 2)
        return (32, 128)[region - 2] * 4 ** (3 - level), False

    def block(region, level, digits):
        count, narrow = extent(region, level)
        if region == ROPE or region == 2:
            place = digits[0] * 16
            for i in range(1, level):
                place = place + digits[i] * 4 ** (2 - i)
            if region == ROPE:
                return rot_ref.at[rope_rows, pl.ds(pl.multiple_of(128 * place, 128), count)]
            return lat_ref.at[pl.ds(pl.multiple_of(6144 + 32 * place, 32), count), cols]
        start = BASES[region] + digits[0] * 768
        if region == 0:
            start = start + (digits[1] * 192 if level > 1 else 0) + (zh * 96 if level > 2 else 0)
        else:
            start = start + (zh * 384 if level > 1 else 0) + (digits[2] * 96 if level > 2 else 0)
        return lat_ref.at[pl.ds(pl.multiple_of(start, 32), count), tile if narrow else cols]

    digits = [tuple(getattr(me, a) for a in o) for o in ORDERS]

    def three(region, level):
        count, narrow = extent(region, level)
        if region == ROPE:
            return rot_ref.at[0:32, 0 : 3 * count]
        return lat_ref.at[0 : 3 * count, 0 : 128 if narrow else 256]

    def gather(region, level):
        ref = block(region, level, digits[region])
        sems = ag_send.at[region * 3 + level - 1], ag_recv.at[region * 3 + level - 1]
        for d in (1, 3, 2):
            send(ref, ref, *sems, beside(ORDERS[region][level - 1], d))
        drains.append((three(region, level), sems[0]))

    def gathered(region, level):
        wait_bytes(three(region, level), ag_recv.at[region * 3 + level - 1])

    def rope_plane():
        ref = block(ROPE, 3, digits[ROPE])
        sems = ag_send.at[ROPE * 3 + 2], ag_recv.at[ROPE * 3 + 2]
        for i in range(4):
            for j in range(4):
                if i or j:
                    send(ref, ref, *sems, me.at(x=(me.x + i) % 4, y=(me.y + j) % 4))
        drains.append((rot_ref.at[0:32, 0:1920], sems[0]))

    def swap(d):
        for region in range(3):
            ref = block(region, 1, ((digits[region][0] + 4 - d) % 4, 0, 0))
            send(ref, ref, sw_send.at[d], sw_recv.at[d], me.at(c=1 - me.c))
        drains.append((lat_ref.at[0:2048, 0:256], sw_send.at[d]))

    def swapped(d):
        wait_bytes(lat_ref.at[0:2048, 0:256], sw_recv.at[d])

    def send_weight(i):
        where = pl.ds(i * CHUNK, CHUNK)
        ref = weight_ref.at[zh, :, where]
        send(weight_hbm.at[:, where], ref, weight_send.at[i], weight_recv.at[i], beside("z", 2))
        drains.append((ref, weight_send.at[i]))

    for region in range(4):
        scatter(region, 0)
    key_copy.start()
    value_copy.start()
    weight_copy.start()
    key_copy.wait()
    latent_queries(0, 16, q_ref, key_ref, qlat_ref)
    for step in range(2):
        for region in (ROPE, 0, 1, 2):
            chosen = pick(region, step)
            landings[2 * (region * 3 + step) + 1][...] = chosen
            scatter(region, step + 1)
        if step == 0:
            send_weight(0)
            latent_queries(16, 32, q_ref, key_ref, qlat_ref)
    for region in (ROPE, 0, 1, 2):
        home = block(region, 3, digits[region])
        home[...] = pick(region, 2)
        if region == ROPE:
            rope_plane()
        else:
            gather(region, 3)
    send_weight(1)
    new_keys(q_ref, new_ref, qlat_ref, acc_ref, max_ref, sum_ref)
    wait_bytes(rot_ref.at[0:32, 0:1920], ag_recv.at[ROPE * 3 + 2])
    gather(ROPE, 1)
    for region in range(3):
        gathered(region, 3)
        gather(region, 2)
    gathered(ROPE, 1)
    send(rot_ref.at[rope_rows], rot_ref.at[rope_rows], sw_send.at[4], sw_recv.at[4], me.at(c=1 - me.c))
    drains.append((rot_ref.at[0:32], sw_send.at[4]))
    for region in range(3):
        gathered(region, 2)
        ref = block(region, 1, digits[region])
        for d in (1, 3, 2):
            send(ref, ref, last_send.at[d - 1], last_recv.at[d - 1], beside(ORDERS[region][0], d))
    for d in (1, 2, 3):
        drains.append((lat_ref.at[0:2048, 0:256], last_send.at[d - 1]))
    swap(0)

    def arrived(d):
        wait_bytes(lat_ref.at[0:2048, 0:256], last_recv.at[d - 1])

    def quarter(d):
        sizes = (768, 768, 512)
        starts = [BASES[r] + sizes[r] * ((digits[r][0] + 4 - d) % 4) for r in range(3)]
        return [pl.ds(pl.multiple_of(s, 256), n) for s, n in zip(starts, sizes)]

    attend = functools.partial(
        attend_rows, q_ref, qlat_ref, lat_ref, rot_ref, acc_ref, max_ref, sum_ref
    )
    def rows_of(i):
        return pl.ds(pl.multiple_of(i * 256, 256), 256)

    wait_bytes(rot_ref.at[0:32], sw_recv.at[4])
    swapped(0)

    @pl.loop(0, 2)
    def _(i):
        attend([(rows_of(2 * i), quarter(0)), (rows_of(2 * i + 1), quarter(0))])

    arrived(1)
    swap(1)
    send_weight(2)
    send_weight(3)
    swapped(1)
    for i in (0, 1):
        attend([(rows_of(2 * i), quarter(1)), (rows_of(2 * i + 1), quarter(1))])
        arrived((3, 2)[i])
        swap((3, 2)[i])
    swapped(3)
    swapped(2)

    def exchange(chunk):
        cols = [pl.ds(chunk * CHUNK + lane * (CHUNK // 2), CHUNK // 2) for lane in (0, 1)]
        whole = pl.ds(chunk * CHUNK, CHUNK)
        sems = [(ex_send.at[chunk * 3 + i], ex_recv.at[chunk * 3 + i]) for i in range(3)]
        for lane, axis in enumerate("xy"):
            ref = att_ref.at[me.x, me.y, :, cols[lane]]
            for d in (1, 3, 2):
                send(ref, ref, *sems[0], beside(axis, d))
        total = att_ref.at[0, 0:3, :, whole]
        drains.append((total, sems[0][0]))
        yield
        wait_bytes(total, sems[0][1])
        lines = [lambda y, s=slice(None): att_ref.at[s, y, :, cols[0]], lambda x, s=slice(None): att_ref.at[x, s, :, cols[1]]]
        for lane, axis in enumerate("yx"):
            ref = lines[lane](getattr(me, axis))
            for d in (1, 3):
                send(ref, ref, *sems[1], beside(axis, d))
        total = att_ref.at[0:2, :, :, whole]
        drains.append((total, sems[1][0]))
        yield
        wait_bytes(total, sems[1][1])
        for lane, axis in enumerate("yx"):
            for d, share in ((1, pl.ds(0, 2)), (3, pl.ds(2, 2))):
                ref = lines[lane]((getattr(me, axis) + 4 - d) % 4, share)
                send(ref, ref, *sems[2], beside(axis, d))
        total = att_ref.at[0:1, :, :, whole]
        drains.append((total, sems[2][0]))
        yield
        wait_bytes(total, sems[2][1])

    def partial_out(chunk, half):
        where = pl.ds(chunk * CHUNK, CHUNK)
        return dot_last(att_ref[:, :, :, where].reshape(512, CHUNK), weight_ref[half, :, where])

    active = []
    for chunk in range(CHUNKS):
        rows = pl.ds(chunk * ROWS, ROWS)
        attend([(rows, quarter(3)), (rows, quarter(2))])
        for other in active[-2:]:
            next(other)
        if chunk == 0:
            value_copy.wait()
        attended_values(chunk, acc_ref, sum_ref, value_ref, att_ref, (me.x, me.y))
        active.append(exchange(chunk))
        next(active[-1])
    weight_copy.wait()
    next(active[2])
    next(active[3])
    for chunk in range(CHUNKS - 1):
        for _ in active[chunk]:
            pass
        wait_bytes(weight_ref.at[zh, :, pl.ds(chunk * CHUNK, CHUNK)], weight_recv.at[chunk])

        @pl.loop(0, 2)
        def _(half):
            term = partial_out(chunk, half)
            total_ref[half] = term if chunk == 0 else total_ref[half] + term

        if chunk == 1:
            next(active[3])
    for _ in active[-1]:
        pass
    wait_bytes(weight_ref.at[zh, :, pl.ds(3 * CHUNK, CHUNK)], weight_recv.at[3])
    for far in (1, 0):
        half = 1 - zh if far else zh
        total_ref[half] = total_ref[half] + partial_out(CHUNKS - 1, half)
        for flip_z in (1, 0):
            for flip_c in (1, 0):
                target_l = 1 - zl if flip_z else zl
                target_c = 1 - me.c if flip_c else me.c
                slot = 4 * far + 2 * flip_z + flip_c
                if slot == 0:
                    continue
                rows = pl.ds(pl.multiple_of((target_l * 2 + target_c) * 128, 128), 128)
                part_ref[slot] = total_ref[half, rows, :].astype(BF)
                send(
                    part_ref.at[slot], land_ref.at[slot], rs_sem.at[0], rs_sem.at[1],
                    me.at(z=half * 2 + target_l, c=target_c),
                )
    wait_bytes(land_ref.at[1:8], rs_sem.at[1])
    drains.append((land_ref.at[1:8], rs_sem.at[0]))
    own_rows = pl.ds(pl.multiple_of((zl * 2 + me.c) * 128, 128), 128)
    for far in (0, 1):
        result = land_ref[4 * far + 1].astype(F32) + land_ref[4 * far + 2].astype(F32)
        result = result + land_ref[4 * far + 3].astype(F32)
        result = result + (land_ref[4].astype(F32) if far else total_ref[zh, own_rows, :])
        out_ref[:, 1 - zh if far else zh] = result.astype(BF).reshape(4, 32, 224)
    for ref, sem in drains:
        wait_bytes(ref, sem)


SCALE = 192**-0.5 * 1.4426950408889634
LAST = (((1,), (1,)), ((), ()))


def dot(a, b):
    return jnp.dot(a, b, preferred_element_type=jnp.float32)


def dot_last(a, b):
    return lax.dot_general(a, b, LAST, preferred_element_type=jnp.float32)


def latent_queries(low, high, q_ref, key_ref, qlat_ref):
    @pl.loop(low, high, unroll=4)
    def _(h):
        rows = pl.ds(pl.multiple_of(h * 32, 32), 32)
        qlat_ref[rows, :] = dot(q_ref[rows, 0:128], key_ref[h]).astype(BF)


def new_keys(q_ref, new_ref, qlat_ref, acc_ref, max_ref, sum_ref):
    @pl.loop(0, CHUNKS)
    def _(r):
        rows = pl.ds(pl.multiple_of(r * ROWS, ROWS), ROWS)
        scores = dot_last(qlat_ref[rows, :], new_ref[:, 0:512])
        scores = (scores + dot_last(q_ref[rows, 128:192], new_ref[:, 512:576])) * SCALE
        row = lax.broadcasted_iota(jnp.int32, (ROWS, 32), 0) % 32
        key = lax.broadcasted_iota(jnp.int32, (ROWS, 32), 1)
        visible = (row // 4 == key // 4) & (key <= row)
        top = jnp.max(jnp.where(visible, scores, -jnp.inf), axis=1, keepdims=True)
        e = jnp.where(visible, jnp.exp2(jnp.where(visible, scores, top) - top), 0.0)
        max_ref[rows, :] = jnp.broadcast_to(top, (ROWS, 128))
        sum_ref[rows, :] = jnp.broadcast_to(jnp.sum(e, axis=1, keepdims=True), (ROWS, 128))
        acc_ref[rows, :] = dot(e.astype(BF), new_ref[:, 0:512])


def attend_rows(q_ref, qlat_ref, lat_ref, rot_ref, acc_ref, max_ref, sum_ref, items):
    scores = [
        [dot_last(qlat_ref[rows, :], lat_ref[keys, :]) + dot(q_ref[rows, 128:192], rot_ref[:, keys]) for keys in key_slices]
        for rows, key_slices in items
    ]
    for (rows, key_slices), parts in zip(items, scores):
        old = max_ref[rows, :]
        top = functools.reduce(jnp.maximum, [jnp.max(s, axis=1, keepdims=True) for s in parts])
        new = jnp.maximum(old, top * SCALE)
        max_ref[rows, :] = new
        shrink = jnp.exp2(old - new)
        total = sum_ref[rows, :] * shrink
        acc = acc_ref[rows, :] * shrink[:, 0:1]
        for s, keys in zip(parts, key_slices):
            e = jnp.exp2(s * SCALE - new[:, 0:1])
            total = total + jnp.sum(e, axis=1, keepdims=True)
            acc = acc + dot(e.astype(BF), lat_ref[keys, :])
        sum_ref[rows, :] = total
        acc_ref[rows, :] = acc


def attended_values(chunk, acc_ref, sum_ref, value_ref, att_ref, place):
    heads = 32 // CHUNKS

    @pl.loop(chunk * heads, (chunk + 1) * heads, unroll=4)
    def _(h):
        rows = pl.ds(pl.multiple_of(h * 32, 32), 32)
        context = (acc_ref[rows, :] / sum_ref[rows, 0:1]).astype(BF)
        cols = pl.ds(pl.multiple_of(h * 128, 128), 128)
        att_ref[place + (slice(None), cols)] = dot(context, value_ref[h]).astype(BF)


def layer(owner_index, queries, new_kv, key_up, value_up, out_weight, latent, rope):
    sem = pltpu.SemaphoreType.DMA
    vm = pltpu.VMEM
    scratch = [
        vm((8192, 512), BF),
        vm((64, 8192), BF),
        vm((32, 128, 512), BF),
        vm((32, 512, 128), BF),
        vm((2, 224, 4096), BF),
        vm((1024, 512), BF),
        vm((1024, 512), F32),
        vm((1024, 128), F32),
        vm((1024, 128), F32),
        vm((4, 4, 32, 4096), BF),
        vm((2, 512, 224), F32),
        vm((8, 128, 224), BF),
        vm((8, 128, 224), BF),
        sem((3,)),
        sem((CHUNKS,)),
        sem((CHUNKS,)),
        sem((12,)),
        sem((12,)),
        sem((12,)),
        sem((12,)),
        sem((12,)),
        sem((3,)),
        sem((3,)),
        sem((5,)),
        sem((5,)),
        sem((3 * CHUNKS,)),
        sem((3 * CHUNKS,)),
        sem((2,)),
    ]
    for slots, held in landing_shapes():
        scratch += [vm(slots, BF), vm(held, BF)]
    hbm = pl.BlockSpec(memory_space=pl.ANY)
    vmem = pl.BlockSpec(memory_space=pltpu.VMEM)
    return pl.pallas_call(
        layer_kernel,
        out_shape=jax.ShapeDtypeStruct((4, 2, 32, 224), BF),
        in_specs=[pl.BlockSpec(memory_space=pltpu.SMEM), vmem, vmem] + [hbm] * 5,
        out_specs=vmem,
        scratch_shapes=scratch,
        compiler_params=pltpu.CompilerParams(
            collective_id=0, has_side_effects=True, vmem_limit_bytes=60 << 20
        ),
        name="layer",
    )(owner_index, queries, new_kv, key_up, value_up, out_weight, latent, rope)


def body(queries, new_kv, owner_index, prefix_latent, prefix_rope, key_up, value_up, out_weight):
    samples, steps, heads, width = queries.shape
    rows = jnp.transpose(queries.reshape(samples * steps, heads, width), (1, 0, 2)).reshape(-1, width)
    out = layer(
        owner_index, rows, new_kv.reshape(samples * steps, -1), key_up, value_up, out_weight.T, prefix_latent[0], prefix_rope[0]
    )
    return out.reshape(64, steps, -1)


def solution(mesh):
    return jax.shard_map(
        body,
        mesh=mesh,
        in_specs=(
            P("grp", None, "tp", None),
            P("grp", None, None),
            P(),
            P("grp", None, None),
            P("grp", None, None),
            P("tp", None, None),
            P("tp", None, None),
            P("tp", "grp"),
        ),
        out_specs=P("tp", None, "grp"),
        check_vma=False,
    )
```

```python
import functools
import jax
import jax.numpy as jnp
from jax import lax
from jax.experimental import pallas as pl
from jax.experimental.pallas import tpu as pltpu
from jax.sharding import PartitionSpec as P

MESH = pl.DeviceIdType.MESH
BF = jnp.bfloat16
F32 = jnp.float32
CHUNKS = 4
CHUNK = 4096 // CHUNKS
ROWS = 1024 // CHUNKS


class Coord:
    def __init__(self):
        g, t = lax.axis_index("grp"), lax.axis_index("tp")
        self.x, self.y, self.z, self.c = g // 8, (g // 2) % 4, (g % 2) * 2 + t // 2, t % 2

    def at(self, **moved):
        x, y, z, c = (moved.get(k, getattr(self, k)) for k in "xyzc")
        return (x * 8 + y * 2 + z // 2, (z % 2) * 2 + c)


ORDERS = (("x", "y", "z"), ("y", "z", "x"), ("z", "x", "y"), ("z", "x", "y"))
BASES = (0, 3072, 6144)
SHARE = ((768, 192, 96), (768, 384, 96), (512, 128, 32), (2048, 128))
ROPE = 3


def landing_shapes():
    shapes = []
    for region in range(4):
        for step in range(2 if region == ROPE else 3):
            share = SHARE[region][step]
            one = (32, share) if region == ROPE else (share, 256 if region == 2 else 128)
            slots = 16 if (region, step) == (ROPE, 1) else 2 if ORDERS[region][step] == "z" else 4
            shapes.append(((slots,) + one, one))
    return shapes


def wait_bytes(ref, sem):
    pltpu.make_async_copy(ref, ref, sem).wait()


def layer_kernel(
    owner_ref, query_ref, fresh_ref, key_hbm, value_hbm, weight_hbm, latent_hbm, rope_hbm, out_ref,
    q_ref, new_ref, wide_ref, lat_ref, rot_ref, key_ref, value_ref, weight_ref, qlat_ref, acc_ref, max_ref, sum_ref,
    att_ref, total_ref, part_ref, land_ref, local_sem, weight_sem, sc_send, sc_recv, sc_own,
    ag_send, ag_recv, last_send, last_recv, sw_send, sw_recv, ex_send, ex_recv, rs_sem, *landings
):
    me = Coord()
    zh, zl = me.z // 2, me.z % 2
    owner = owner_ref[0]
    owner_digit = {"x": owner // 8, "y": (owner // 2) % 4, "z": owner % 2}
    key_copy = pltpu.make_async_copy(key_hbm, key_ref, local_sem.at[0])
    value_copy = pltpu.make_async_copy(value_hbm, value_ref, local_sem.at[1])
    weight_copy = pltpu.make_async_copy(weight_hbm, weight_ref.at[zh], local_sem.at[2])
    drains = []

    def send(src, dst, send_sem, recv_sem, device):
        copy = pltpu.make_async_remote_copy(
            src_ref=src, dst_ref=dst, send_sem=send_sem, recv_sem=recv_sem, device_id=device, device_id_type=MESH
        )
        copy.start()
        return copy

    def beside(axis, d):
        return me.at(**{axis: (getattr(me, axis) + d) % 4})

    barrier = pltpu.get_barrier_semaphore()
    peers = [beside(a, d) for a in "xyz" for d in (1, 2, 3)]
    peers += [me.at(z=(me.z + d) % 4, c=1 - me.c) for d in range(4)]
    peers += [me.at(x=(me.x + i) % 4, y=(me.y + j) % 4) for i in (1, 2, 3) for j in (1, 2, 3)]
    for peer in peers:
        pl.semaphore_signal(barrier, inc=1, device_id=peer, device_id_type=MESH)
    pl.semaphore_wait(barrier, len(peers))

    cols = pl.ds(pl.multiple_of(256 * me.c, 256), 256)
    rope_rows = pl.ds(pl.multiple_of(32 * me.c, 32), 32)

    def own_digit(axis):
        return zh if axis == "z" else getattr(me, axis)

    tile = pl.ds(pl.multiple_of(256 * me.c + 128 * zl, 128), 128)

    def source(region, digit):
        if region == ROPE:
            return rope_hbm.at[rope_rows, pl.ds(pl.multiple_of(4096 * digit + 2048 * zl, 128), 2048)]
        if region == 2:
            return latent_hbm.at[pl.ds(pl.multiple_of(6144 + 1024 * digit + 512 * zl, 512), 512), cols]
        return latent_hbm.at[pl.ds(pl.multiple_of(BASES[region] + 768 * digit, 256), 768), tile]

    def part(region, step, digit):
        if step == 0:
            return source(region, digit)
        held = landings[2 * (region * 3 + step - 1) + 1]
        share = SHARE[region][step]
        if region == ROPE:
            return held.at[:, pl.ds(pl.multiple_of(digit * share, 128), share)]
        return held.at[pl.ds(pl.multiple_of(digit * share, 32), share)]

    def scatter(region, step):
        axis = ORDERS[region][step]
        index = region * 3 + step
        slots = landings[2 * index]
        mine = own_digit(axis)
        if axis == "z":
            send(part(region, step, 1 - zh), slots.at[mine], sc_send.at[index], sc_recv.at[index], beside("z", 2))
        else:
            for d in (1, 3, 2):
                digit = (mine + d) % 4
                send(part(region, step, digit), slots.at[mine], sc_send.at[index], sc_recv.at[index], beside(axis, d))
        pltpu.make_async_copy(part(region, step, mine), slots.at[mine], sc_own.at[index]).start()
        others = slots.at[pl.ds(0, slots.shape[0] - 1)]
        drains.append((others, sc_send.at[index]))

    def pick(region, step):
        index = region * 3 + step
        slots = landings[2 * index]
        wait_bytes(slots.at[0], sc_own.at[index])
        wait_bytes(slots.at[pl.ds(0, slots.shape[0] - 1)], sc_recv.at[index])
        return slots[owner_digit[ORDERS[region][step]]]

    def extent(region, level):
        if region in (0, 1):
            return (768, (192, 384)[region], 96)[level - 1], level == 3 or (region, level) == (1, 2)
        return (32, 128)[region - 2] * 4 ** (3 - level), False

    def block(region, level, digits):
        count, narrow = extent(region, level)
        if region == ROPE or region == 2:
            place = digits[0] * 16
            for i in range(1, level):
                place = place + digits[i] * 4 ** (2 - i)
            if region == ROPE:
                return rot_ref.at[rope_rows, pl.ds(pl.multiple_of(128 * place, 128), count)]
            return lat_ref.at[pl.ds(pl.multiple_of(6144 + 32 * place, 32), count), cols]
        start = BASES[region] + digits[0] * 768
        if region == 0:
            start = start + (digits[1] * 192 if level > 1 else 0) + (zh * 96 if level > 2 else 0)
        else:
            start = start + (zh * 384 if level > 1 else 0) + (digits[2] * 96 if level > 2 else 0)
        return lat_ref.at[pl.ds(pl.multiple_of(start, 32), count), tile if narrow else cols]

    digits = [tuple(getattr(me, a) for a in o) for o in ORDERS]

    def three(region, level):
        count, narrow = extent(region, level)
        if region == ROPE:
            return rot_ref.at[0:32, 0 : 3 * count]
        return lat_ref.at[0 : 3 * count, 0 : 128 if narrow else 256]

    def gather(region, level):
        ref = block(region, level, digits[region])
        sems = ag_send.at[region * 3 + level - 1], ag_recv.at[region * 3 + level - 1]
        for d in (1, 3, 2):
            send(ref, ref, *sems, beside(ORDERS[region][level - 1], d))
        drains.append((three(region, level), sems[0]))

    def gathered(region, level):
        wait_bytes(three(region, level), ag_recv.at[region * 3 + level - 1])

    plane = [(i, j) for i in range(4) for j in range(4) if i or j]

    def rope_scatter():
        held, slots = landings[2 * 9 + 1], landings[2 * 10]
        mine = me.x * 4 + me.y
        for i, j in plane:
            x, y = (me.x + i) % 4, (me.y + j) % 4
            lanes = pl.ds(pl.multiple_of(128 * (x * 4 + y), 128), 128)
            send(held.at[:, lanes], slots.at[mine], sc_send.at[10], sc_recv.at[10], me.at(x=x, y=y))
        lanes = pl.ds(pl.multiple_of(128 * mine, 128), 128)
        pltpu.make_async_copy(held.at[:, lanes], slots.at[mine], sc_own.at[10]).start()
        drains.append((slots.at[0:15], sc_send.at[10]))

    def rope_pick():
        slots = landings[2 * 10]
        wait_bytes(slots.at[0], sc_own.at[10])
        wait_bytes(slots.at[0:15], sc_recv.at[10])
        return slots[owner_digit["x"] * 4 + owner_digit["y"]]

    def rope_plane():
        ref = block(ROPE, 3, digits[ROPE])
        sems = ag_send.at[ROPE * 3 + 2], ag_recv.at[ROPE * 3 + 2]
        for i, j in plane:
            send(ref, ref, *sems, me.at(x=(me.x + i) % 4, y=(me.y + j) % 4))
        drains.append((rot_ref.at[0:32, 0:1920], sems[0]))

    def swap(d):
        for region in range(3):
            ref = block(region, 1, ((digits[region][0] + 4 - d) % 4, 0, 0))
            send(ref, ref, sw_send.at[d], sw_recv.at[d], me.at(c=1 - me.c))
        drains.append((lat_ref.at[0:2048, 0:256], sw_send.at[d]))

    def swapped(d):
        wait_bytes(lat_ref.at[0:2048, 0:256], sw_recv.at[d])

    def send_weight(low, high):
        where = pl.ds(16 * low, 16 * (high - low))
        send(weight_hbm.at[where], weight_ref.at[zh, where], weight_sem.at[0], weight_sem.at[1], beside("z", 2))

    for region in range(4):
        scatter(region, 0)
    key_copy.start()
    value_copy.start()
    weight_copy.start()
    wide_ref[...] = query_ref[...].astype(F32)

    @pl.loop(0, 32, unroll=4)
    def _(h):
        q_ref[pl.ds(pl.multiple_of(h * 32, 32), 32), :] = wide_ref[:, h, :].astype(BF)

    for sample in range(8):
        wide_ref[0, 4 * sample : 4 * sample + 4, :] = fresh_ref[sample, :, 0:192].astype(F32)
        wide_ref[1, 4 * sample : 4 * sample + 4, :] = fresh_ref[sample, :, 192:384].astype(F32)
        wide_ref[2, 4 * sample : 4 * sample + 4, :] = fresh_ref[sample, :, 384:576].astype(F32)
    for third in range(3):
        new_ref[:, 192 * third : 192 * third + 192] = wide_ref[third].astype(BF)
    key_copy.wait()
    latent_queries(0, 16, q_ref, key_ref, qlat_ref)
    landings[2 * 9 + 1][...] = pick(ROPE, 0)
    rope_scatter()
    for region in range(3):
        landings[2 * (region * 3) + 1][...] = pick(region, 0)
        scatter(region, 1)
    send_weight(0, 1)
    latent_queries(16, 32, q_ref, key_ref, qlat_ref)
    home = block(ROPE, 3, digits[ROPE])
    home[...] = rope_pick()
    rope_plane()
    for region in range(3):
        landings[2 * (region * 3 + 1) + 1][...] = pick(region, 1)
        scatter(region, 2)
    send_weight(1, 2)
    wait_bytes(rot_ref.at[0:32, 0:1920], ag_recv.at[ROPE * 3 + 2])
    for region in range(3):
        home = block(region, 3, digits[region])
        home[...] = pick(region, 2)
        gather(region, 3)
    gather(ROPE, 1)
    new_keys(q_ref, new_ref, qlat_ref, acc_ref, max_ref, sum_ref)
    for region in range(3):
        gathered(region, 3)
        gather(region, 2)
    gathered(ROPE, 1)
    send(rot_ref.at[rope_rows], rot_ref.at[rope_rows], sw_send.at[4], sw_recv.at[4], me.at(c=1 - me.c))
    drains.append((rot_ref.at[0:32], sw_send.at[4]))
    send_weight(2, 3)
    for region in range(3):
        gathered(region, 2)
        ref = block(region, 1, digits[region])
        for d in (1, 3, 2):
            send(ref, ref, last_send.at[d - 1], last_recv.at[d - 1], beside(ORDERS[region][0], d))
    for d in (1, 2, 3):
        drains.append((lat_ref.at[0:2048, 0:256], last_send.at[d - 1]))
    swap(0)

    def arrived(d):
        wait_bytes(lat_ref.at[0:2048, 0:256], last_recv.at[d - 1])

    def quarter(d):
        sizes = (768, 768, 512)
        starts = [BASES[r] + sizes[r] * ((digits[r][0] + 4 - d) % 4) for r in range(3)]
        return [pl.ds(pl.multiple_of(s, 256), n) for s, n in zip(starts, sizes)]

    attend = functools.partial(
        attend_rows, q_ref, qlat_ref, lat_ref, rot_ref, acc_ref, max_ref, sum_ref
    )
    def rows_of(i):
        return pl.ds(pl.multiple_of(i * 256, 256), 256)

    wait_bytes(rot_ref.at[0:32], sw_recv.at[4])
    swapped(0)

    def half(i, d):
        attend([(rows_of(2 * i), quarter(d)), (rows_of(2 * i + 1), quarter(d))])

    half(0, 0)
    arrived(1)
    swap(1)
    half(1, 0)
    swapped(1)
    half(0, 1)
    arrived(3)
    swap(3)
    arrived(2)
    swap(2)
    send_weight(3, 5)
    half(1, 1)
    swapped(3)
    swapped(2)
    send_weight(5, 14)
    drains.append((weight_ref.at[zh], weight_sem.at[0]))

    def exchange(chunk):
        cols = [pl.ds(chunk * CHUNK + lane * (CHUNK // 2), CHUNK // 2) for lane in (0, 1)]
        whole = pl.ds(chunk * CHUNK, CHUNK)
        sems = [(ex_send.at[chunk * 3 + i], ex_recv.at[chunk * 3 + i]) for i in range(3)]
        for lane, axis in enumerate("xy"):
            ref = att_ref.at[me.x, me.y, :, cols[lane]]
            for d in (1, 3, 2):
                send(ref, ref, *sems[0], beside(axis, d))
        total = att_ref.at[0, 0:3, :, whole]
        drains.append((total, sems[0][0]))
        yield
        wait_bytes(total, sems[0][1])
        lines = [lambda y, s=slice(None): att_ref.at[s, y, :, cols[0]], lambda x, s=slice(None): att_ref.at[x, s, :, cols[1]]]
        for lane, axis in enumerate("yx"):
            ref = lines[lane](getattr(me, axis))
            for d in (1, 3) if chunk < CHUNKS - 1 else (1, 3, 2):
                send(ref, ref, *sems[1], beside(axis, d))
        total = att_ref.at[0 : 2 if chunk < CHUNKS - 1 else 3, :, :, whole]
        drains.append((total, sems[1][0]))
        yield
        wait_bytes(total, sems[1][1])
        if chunk == CHUNKS - 1:
            return
        for lane, axis in enumerate("yx"):
            for d, share in ((1, pl.ds(0, 2)), (3, pl.ds(2, 2))):
                ref = lines[lane]((getattr(me, axis) + 4 - d) % 4, share)
                send(ref, ref, *sems[2], beside(axis, d))
        total = att_ref.at[0:1, :, :, whole]
        drains.append((total, sems[2][0]))
        yield
        wait_bytes(total, sems[2][1])

    def partial_out(chunk, half):
        where = pl.ds(chunk * CHUNK, CHUNK)
        return dot_last(att_ref[:, :, :, where].reshape(512, CHUNK), weight_ref[half, :, where])

    active = []
    for chunk in range(CHUNKS):
        rows = pl.ds(chunk * ROWS, ROWS)
        attend([(rows, quarter(3)), (rows, quarter(2))])
        for other in active[-2:]:
            next(other)
        if chunk == 0:
            value_copy.wait()
        attended_values(chunk, acc_ref, sum_ref, value_ref, att_ref, (me.x, me.y))
        active.append(exchange(chunk))
        next(active[-1])
    weight_copy.wait()
    next(active[2])
    next(active[3])
    for chunk in range(CHUNKS - 1):
        for _ in active[chunk]:
            pass
        if chunk == 0:
            wait_bytes(weight_ref.at[zh], weight_sem.at[1])

        @pl.loop(0, 2)
        def _(half):
            term = partial_out(chunk, half)
            total_ref[half] = term if chunk == 0 else total_ref[half] + term
    for _ in active[-1]:
        pass
    for far in (1, 0):
        half = 1 - zh if far else zh
        total_ref[half] = total_ref[half] + partial_out(CHUNKS - 1, half)
        for flip_z in (1, 0):
            for flip_c in (1, 0):
                target_l = 1 - zl if flip_z else zl
                target_c = 1 - me.c if flip_c else me.c
                slot = 4 * far + 2 * flip_z + flip_c
                if slot == 0:
                    continue
                rows = pl.ds(pl.multiple_of((target_l * 2 + target_c) * 128, 128), 128)
                part_ref[slot] = total_ref[half, rows, :].astype(BF)
                send(
                    part_ref.at[slot], land_ref.at[slot], rs_sem.at[0], rs_sem.at[1],
                    me.at(z=half * 2 + target_l, c=target_c),
                )
    wait_bytes(land_ref.at[1:8], rs_sem.at[1])
    drains.append((land_ref.at[1:8], rs_sem.at[0]))
    own_rows = pl.ds(pl.multiple_of((zl * 2 + me.c) * 128, 128), 128)
    for far in (0, 1):
        result = land_ref[4 * far + 1].astype(F32) + land_ref[4 * far + 2].astype(F32)
        result = result + land_ref[4 * far + 3].astype(F32)
        result = result + (land_ref[4].astype(F32) if far else total_ref[zh, own_rows, :])
        out_ref[:, 1 - zh if far else zh] = result.astype(BF).reshape(4, 32, 224)
    for ref, sem in drains:
        wait_bytes(ref, sem)


SCALE = 192**-0.5 * 1.4426950408889634
LAST = (((1,), (1,)), ((), ()))


def dot(a, b):
    return jnp.dot(a, b, preferred_element_type=jnp.float32)


def dot_last(a, b):
    return lax.dot_general(a, b, LAST, preferred_element_type=jnp.float32)


def latent_queries(low, high, q_ref, key_ref, qlat_ref):
    @pl.loop(low, high, unroll=4)
    def _(h):
        rows = pl.ds(pl.multiple_of(h * 32, 32), 32)
        qlat_ref[rows, :] = dot(q_ref[rows, 0:128], key_ref[h]).astype(BF)


def new_keys(q_ref, new_ref, qlat_ref, acc_ref, max_ref, sum_ref):
    @pl.loop(0, CHUNKS)
    def _(r):
        rows = pl.ds(pl.multiple_of(r * ROWS, ROWS), ROWS)
        scores = dot_last(qlat_ref[rows, :], new_ref[:, 0:512])
        scores = (scores + dot_last(q_ref[rows, 128:192], new_ref[:, 512:576])) * SCALE
        row = lax.broadcasted_iota(jnp.int32, (ROWS, 32), 0) % 32
        key = lax.broadcasted_iota(jnp.int32, (ROWS, 32), 1)
        visible = (row // 4 == key // 4) & (key <= row)
        top = jnp.max(jnp.where(visible, scores, -jnp.inf), axis=1, keepdims=True)
        e = jnp.where(visible, jnp.exp2(jnp.where(visible, scores, top) - top), 0.0)
        max_ref[rows, :] = jnp.broadcast_to(top, (ROWS, 128))
        sum_ref[rows, :] = jnp.broadcast_to(jnp.sum(e, axis=1, keepdims=True), (ROWS, 128))
        acc_ref[rows, :] = dot(e.astype(BF), new_ref[:, 0:512])


def attend_rows(q_ref, qlat_ref, lat_ref, rot_ref, acc_ref, max_ref, sum_ref, items):
    scores = [
        [dot_last(qlat_ref[rows, :], lat_ref[keys, :]) + dot(q_ref[rows, 128:192], rot_ref[:, keys]) for keys in key_slices]
        for rows, key_slices in items
    ]
    for (rows, key_slices), parts in zip(items, scores):
        old = max_ref[rows, :]
        top = functools.reduce(jnp.maximum, [jnp.max(s, axis=1, keepdims=True) for s in parts])
        new = jnp.maximum(old, top * SCALE)
        max_ref[rows, :] = new
        shrink = jnp.exp2(old - new)
        total = sum_ref[rows, :] * shrink
        acc = acc_ref[rows, :] * shrink[:, 0:1]
        for s, keys in zip(parts, key_slices):
            e = jnp.exp2(s * SCALE - new[:, 0:1])
            total = total + jnp.sum(e, axis=1, keepdims=True)
            acc = acc + dot(e.astype(BF), lat_ref[keys, :])
        sum_ref[rows, :] = total
        acc_ref[rows, :] = acc


def attended_values(chunk, acc_ref, sum_ref, value_ref, att_ref, place):
    heads = 32 // CHUNKS

    @pl.loop(chunk * heads, (chunk + 1) * heads, unroll=4)
    def _(h):
        rows = pl.ds(pl.multiple_of(h * 32, 32), 32)
        context = (acc_ref[rows, :] / sum_ref[rows, 0:1]).astype(BF)
        cols = pl.ds(pl.multiple_of(h * 128, 128), 128)
        att_ref[place + (slice(None), cols)] = dot(context, value_ref[h]).astype(BF)


def layer(owner_index, queries, new_kv, key_up, value_up, out_weight, latent, rope):
    sem = pltpu.SemaphoreType.DMA
    vm = pltpu.VMEM
    scratch = [
        vm((1024, 192), BF),
        vm((32, 576), BF),
        vm((32, 32, 192), F32),
        vm((8192, 512), BF),
        vm((64, 8192), BF),
        vm((32, 128, 512), BF),
        vm((32, 512, 128), BF),
        vm((2, 224, 4096), BF),
        vm((1024, 512), BF),
        vm((1024, 512), F32),
        vm((1024, 128), F32),
        vm((1024, 128), F32),
        vm((4, 4, 32, 4096), BF),
        vm((2, 512, 224), F32),
        vm((8, 128, 224), BF),
        vm((8, 128, 224), BF),
        sem((3,)),
        sem((2,)),
        sem((12,)),
        sem((12,)),
        sem((12,)),
        sem((12,)),
        sem((12,)),
        sem((3,)),
        sem((3,)),
        sem((5,)),
        sem((5,)),
        sem((3 * CHUNKS,)),
        sem((3 * CHUNKS,)),
        sem((2,)),
    ]
    for slots, held in landing_shapes():
        scratch += [vm(slots, BF), vm(held, BF)]
    hbm = pl.BlockSpec(memory_space=pl.ANY)
    vmem = pl.BlockSpec(memory_space=pltpu.VMEM)
    return pl.pallas_call(
        layer_kernel,
        out_shape=jax.ShapeDtypeStruct((4, 2, 32, 224), BF),
        in_specs=[pl.BlockSpec(memory_space=pltpu.SMEM), vmem, vmem] + [hbm] * 5,
        out_specs=vmem,
        scratch_shapes=scratch,
        compiler_params=pltpu.CompilerParams(
            collective_id=0, has_side_effects=True, vmem_limit_bytes=60 << 20
        ),
        name="layer",
    )(owner_index, queries, new_kv, key_up, value_up, out_weight, latent, rope)


def body(queries, new_kv, owner_index, prefix_latent, prefix_rope, key_up, value_up, out_weight):
    samples, steps, heads, width = queries.shape
    out = layer(
        owner_index, queries.reshape(samples * steps, heads, width), new_kv, key_up, value_up, out_weight.T,
        prefix_latent[0], prefix_rope[0],
    )
    return out.reshape(64, steps, -1)


def solution(mesh):
    return jax.shard_map(
        body,
        mesh=mesh,
        in_specs=(
            P("grp", None, "tp", None),
            P("grp", None, None),
            P(),
            P("grp", None, None),
            P("grp", None, None),
            P("tp", None, None),
            P("tp", None, None),
            P("tp", "grp"),
        ),
        out_specs=P("tp", None, "grp"),
        check_vma=False,
    )
```

```python
import functools
import jax
import jax.numpy as jnp
from jax import lax
from jax.experimental import pallas as pl
from jax.experimental.pallas import tpu as pltpu
from jax.sharding import PartitionSpec as P

MESH = pl.DeviceIdType.MESH
BF = jnp.bfloat16
F32 = jnp.float32
CHUNKS = 4
CHUNK = 4096 // CHUNKS
ROWS = 1024 // CHUNKS


class Coord:
    def __init__(self):
        g, t = lax.axis_index("grp"), lax.axis_index("tp")
        self.x, self.y, self.z, self.c = g // 8, (g // 2) % 4, (g % 2) * 2 + t // 2, t % 2

    def at(self, **moved):
        x, y, z, c = (moved.get(k, getattr(self, k)) for k in "xyzc")
        return (x * 8 + y * 2 + z // 2, (z % 2) * 2 + c)


ORDERS = (("x", "y", "z"), ("y", "z", "x"), ("z", "x", "y"), ("z", "x", "y"))
BASES = (0, 3072, 6144)
SHARE = ((768, 192, 96), (768, 384, 96), (512, 128, 32), (2048, 128))
ROPE = 3


def landing_shapes():
    shapes = []
    for region in range(4):
        for step in range(2 if region == ROPE else 3):
            share = SHARE[region][step]
            one = (32, share) if region == ROPE else (share, 256 if region == 2 else 128)
            slots = 16 if (region, step) == (ROPE, 1) else 2 if ORDERS[region][step] == "z" else 4
            shapes.append(((slots,) + one, one))
    return shapes


def wait_bytes(ref, sem):
    pltpu.make_async_copy(ref, ref, sem).wait()


def layer_kernel(
    owner_ref, query_ref, fresh_ref, key_hbm, value_hbm, weight_hbm, latent_hbm, rope_hbm, out_ref,
    q_ref, new_ref, wide_ref, lat_ref, rot_ref, key_ref, value_ref, weight_ref, qlat_ref, acc_ref, max_ref, sum_ref,
    att_ref, total_ref, part_ref, land_ref, local_sem, weight_sem, sc_send, sc_recv, sc_own,
    ag_send, ag_recv, last_send, last_recv, sw_send, sw_recv, ex_send, ex_recv, rs_sem, *landings
):
    me = Coord()
    zh, zl = me.z // 2, me.z % 2
    owner = owner_ref[0]
    owner_digit = {"x": owner // 8, "y": (owner // 2) % 4, "z": owner % 2}
    key_copy = pltpu.make_async_copy(key_hbm, key_ref, local_sem.at[0])
    value_copy = pltpu.make_async_copy(value_hbm, value_ref, local_sem.at[1])
    weight_copy = pltpu.make_async_copy(weight_hbm, weight_ref.at[zh], local_sem.at[2])
    drains = []

    def send(src, dst, send_sem, recv_sem, device):
        copy = pltpu.make_async_remote_copy(
            src_ref=src, dst_ref=dst, send_sem=send_sem, recv_sem=recv_sem, device_id=device, device_id_type=MESH
        )
        copy.start()
        return copy

    def beside(axis, d):
        return me.at(**{axis: (getattr(me, axis) + d) % 4})

    barrier = pltpu.get_barrier_semaphore()
    peers = [beside(a, d) for a in "xyz" for d in (1, 2, 3)]
    peers += [me.at(z=(me.z + d) % 4, c=1 - me.c) for d in range(4)]
    peers += [me.at(x=(me.x + i) % 4, y=(me.y + j) % 4) for i in (1, 2, 3) for j in (1, 2, 3)]
    for peer in peers:
        pl.semaphore_signal(barrier, inc=1, device_id=peer, device_id_type=MESH)
    pl.semaphore_wait(barrier, len(peers))

    cols = pl.ds(pl.multiple_of(256 * me.c, 256), 256)
    rope_rows = pl.ds(pl.multiple_of(32 * me.c, 32), 32)

    def own_digit(axis):
        return zh if axis == "z" else getattr(me, axis)

    tile = pl.ds(pl.multiple_of(256 * me.c + 128 * zl, 128), 128)

    def source(region, digit):
        if region == ROPE:
            return rope_hbm.at[rope_rows, pl.ds(pl.multiple_of(4096 * digit + 2048 * zl, 128), 2048)]
        if region == 2:
            return latent_hbm.at[pl.ds(pl.multiple_of(6144 + 1024 * digit + 512 * zl, 512), 512), cols]
        return latent_hbm.at[pl.ds(pl.multiple_of(BASES[region] + 768 * digit, 256), 768), tile]

    def part(region, step, digit):
        if step == 0:
            return source(region, digit)
        held = landings[2 * (region * 3 + step - 1) + 1]
        share = SHARE[region][step]
        if region == ROPE:
            return held.at[:, pl.ds(pl.multiple_of(digit * share, 128), share)]
        return held.at[pl.ds(pl.multiple_of(digit * share, 32), share)]

    def scatter(region, step):
        axis = ORDERS[region][step]
        index = region * 3 + step
        slots = landings[2 * index]
        mine = own_digit(axis)
        if axis == "z":
            send(part(region, step, 1 - zh), slots.at[mine], sc_send.at[index], sc_recv.at[index], beside("z", 2))
        else:
            for d in (1, 3, 2):
                digit = (mine + d) % 4
                send(part(region, step, digit), slots.at[mine], sc_send.at[index], sc_recv.at[index], beside(axis, d))
        pltpu.make_async_copy(part(region, step, mine), slots.at[mine], sc_own.at[index]).start()
        others = slots.at[pl.ds(0, slots.shape[0] - 1)]
        drains.append((others, sc_send.at[index]))

    def pick(region, step):
        index = region * 3 + step
        slots = landings[2 * index]
        wait_bytes(slots.at[0], sc_own.at[index])
        wait_bytes(slots.at[pl.ds(0, slots.shape[0] - 1)], sc_recv.at[index])
        return slots[owner_digit[ORDERS[region][step]]]

    def extent(region, level):
        if region in (0, 1):
            return (768, (192, 384)[region], 96)[level - 1], level == 3 or (region, level) == (1, 2)
        return (32, 128)[region - 2] * 4 ** (3 - level), False

    def block(region, level, digits):
        count, narrow = extent(region, level)
        if region == ROPE or region == 2:
            place = digits[0] * 16
            for i in range(1, level):
                place = place + digits[i] * 4 ** (2 - i)
            if region == ROPE:
                return rot_ref.at[rope_rows, pl.ds(pl.multiple_of(128 * place, 128), count)]
            return lat_ref.at[pl.ds(pl.multiple_of(6144 + 32 * place, 32), count), cols]
        start = BASES[region] + digits[0] * 768
        if region == 0:
            start = start + (digits[1] * 192 if level > 1 else 0) + (zh * 96 if level > 2 else 0)
        else:
            start = start + (zh * 384 if level > 1 else 0) + (digits[2] * 96 if level > 2 else 0)
        return lat_ref.at[pl.ds(pl.multiple_of(start, 32), count), tile if narrow else cols]

    digits = [tuple(getattr(me, a) for a in o) for o in ORDERS]

    def three(region, level):
        count, narrow = extent(region, level)
        if region == ROPE:
            return rot_ref.at[0:32, 0 : 3 * count]
        return lat_ref.at[0 : 3 * count, 0 : 128 if narrow else 256]

    def gather(region, level):
        ref = block(region, level, digits[region])
        sems = ag_send.at[region * 3 + level - 1], ag_recv.at[region * 3 + level - 1]
        for d in (1, 3, 2):
            send(ref, ref, *sems, beside(ORDERS[region][level - 1], d))
        drains.append((three(region, level), sems[0]))

    def gathered(region, level):
        wait_bytes(three(region, level), ag_recv.at[region * 3 + level - 1])

    plane = [(i, j) for i in range(4) for j in range(4) if i or j]

    def rope_scatter():
        held, slots = landings[2 * 9 + 1], landings[2 * 10]
        mine = me.x * 4 + me.y
        for i, j in plane:
            x, y = (me.x + i) % 4, (me.y + j) % 4
            lanes = pl.ds(pl.multiple_of(128 * (x * 4 + y), 128), 128)
            send(held.at[:, lanes], slots.at[mine], sc_send.at[10], sc_recv.at[10], me.at(x=x, y=y))
        lanes = pl.ds(pl.multiple_of(128 * mine, 128), 128)
        pltpu.make_async_copy(held.at[:, lanes], slots.at[mine], sc_own.at[10]).start()
        drains.append((slots.at[0:15], sc_send.at[10]))

    def rope_pick():
        slots = landings[2 * 10]
        wait_bytes(slots.at[0], sc_own.at[10])
        wait_bytes(slots.at[0:15], sc_recv.at[10])
        return slots[owner_digit["x"] * 4 + owner_digit["y"]]

    def rope_plane():
        ref = block(ROPE, 3, digits[ROPE])
        sems = ag_send.at[ROPE * 3 + 2], ag_recv.at[ROPE * 3 + 2]
        for i, j in plane:
            send(ref, ref, *sems, me.at(x=(me.x + i) % 4, y=(me.y + j) % 4))
        drains.append((rot_ref.at[0:32, 0:1920], sems[0]))

    def swap(d):
        for region in range(3):
            ref = block(region, 1, ((digits[region][0] + 4 - d) % 4, 0, 0))
            send(ref, ref, sw_send.at[d], sw_recv.at[d], me.at(c=1 - me.c))
        drains.append((lat_ref.at[0:2048, 0:256], sw_send.at[d]))

    def swapped(d):
        wait_bytes(lat_ref.at[0:2048, 0:256], sw_recv.at[d])

    def send_weight(low, high):
        where = pl.ds(16 * low, 16 * (high - low))
        send(weight_hbm.at[where], weight_ref.at[zh, where], weight_sem.at[0], weight_sem.at[1], beside("z", 2))

    def last(region, distances):
        ref = block(region, 1, digits[region])
        for d in distances:
            send(ref, ref, last_send.at[d - 1], last_recv.at[d - 1], beside(ORDERS[region][0], d))

    for region in range(4):
        scatter(region, 0)
    key_copy.start()
    value_copy.start()
    weight_copy.start()
    wide_ref[...] = query_ref[...].astype(F32)

    @pl.loop(0, 32, unroll=4)
    def _(h):
        q_ref[pl.ds(pl.multiple_of(h * 32, 32), 32), :] = wide_ref[:, h, :].astype(BF)

    for sample in range(8):
        wide_ref[0, 4 * sample : 4 * sample + 4, :] = fresh_ref[sample, :, 0:192].astype(F32)
        wide_ref[1, 4 * sample : 4 * sample + 4, :] = fresh_ref[sample, :, 192:384].astype(F32)
        wide_ref[2, 4 * sample : 4 * sample + 4, :] = fresh_ref[sample, :, 384:576].astype(F32)
    for third in range(3):
        new_ref[:, 192 * third : 192 * third + 192] = wide_ref[third].astype(BF)
    key_copy.wait()
    latent_queries(0, 16, q_ref, key_ref, qlat_ref)
    landings[2 * 9 + 1][...] = pick(ROPE, 0)
    rope_scatter()
    for region in range(3):
        landings[2 * (region * 3) + 1][...] = pick(region, 0)
        scatter(region, 1)
    send_weight(0, 1)
    latent_queries(16, 32, q_ref, key_ref, qlat_ref)
    home = block(ROPE, 3, digits[ROPE])
    home[...] = rope_pick()
    rope_plane()
    for region in range(3):
        landings[2 * (region * 3 + 1) + 1][...] = pick(region, 1)
        scatter(region, 2)
    send_weight(1, 2)
    wait_bytes(rot_ref.at[0:32, 0:1920], ag_recv.at[ROPE * 3 + 2])
    for region in range(3):
        home = block(region, 3, digits[region])
        home[...] = pick(region, 2)
        gather(region, 3)
    gather(ROPE, 1)
    new_keys(q_ref, new_ref, qlat_ref, acc_ref, max_ref, sum_ref)
    for region in range(3):
        gathered(region, 3)
        gather(region, 2)
    gathered(ROPE, 1)
    send(rot_ref.at[rope_rows], rot_ref.at[rope_rows], sw_send.at[4], sw_recv.at[4], me.at(c=1 - me.c))
    drains.append((rot_ref.at[0:32], sw_send.at[4]))
    send_weight(2, 3)
    for region in range(3):
        gathered(region, 2)
        last(region, (1, 3))
    for d in (1, 2, 3):
        drains.append((lat_ref.at[0:2048, 0:256], last_send.at[d - 1]))
    swap(0)

    def arrived(d):
        wait_bytes(lat_ref.at[0:2048, 0:256], last_recv.at[d - 1])

    def quarter(d):
        sizes = (768, 768, 512)
        starts = [BASES[r] + sizes[r] * ((digits[r][0] + 4 - d) % 4) for r in range(3)]
        return [pl.ds(pl.multiple_of(s, 256), n) for s, n in zip(starts, sizes)]

    attend = functools.partial(
        attend_rows, q_ref, qlat_ref, lat_ref, rot_ref, acc_ref, max_ref, sum_ref
    )
    def rows_of(i):
        return pl.ds(pl.multiple_of(i * 256, 256), 256)

    wait_bytes(rot_ref.at[0:32], sw_recv.at[4])
    swapped(0)

    def half(i, d):
        attend([(rows_of(2 * i), quarter(d)), (rows_of(2 * i + 1), quarter(d))])

    half(0, 0)
    for region in range(3):
        last(region, (2,))
    half(1, 0)
    arrived(1)
    swap(1)
    arrived(3)
    swap(3)
    swapped(1)
    half(0, 1)
    arrived(2)
    swap(2)
    send_weight(3, 5)
    half(1, 1)
    swapped(3)
    swapped(2)
    send_weight(5, 14)
    drains.append((weight_ref.at[zh], weight_sem.at[0]))

    def exchange(chunk):
        cols = [pl.ds(chunk * CHUNK + lane * (CHUNK // 2), CHUNK // 2) for lane in (0, 1)]
        whole = pl.ds(chunk * CHUNK, CHUNK)
        sems = [(ex_send.at[chunk * 3 + i], ex_recv.at[chunk * 3 + i]) for i in range(3)]
        for lane, axis in enumerate("xy"):
            ref = att_ref.at[me.x, me.y, :, cols[lane]]
            for d in (1, 3, 2):
                send(ref, ref, *sems[0], beside(axis, d))
        total = att_ref.at[0, 0:3, :, whole]
        drains.append((total, sems[0][0]))
        yield
        wait_bytes(total, sems[0][1])
        lines = [lambda y, s=slice(None): att_ref.at[s, y, :, cols[0]], lambda x, s=slice(None): att_ref.at[x, s, :, cols[1]]]
        for lane, axis in enumerate("yx"):
            ref = lines[lane](getattr(me, axis))
            for d in (1, 3) if chunk < CHUNKS - 1 else (1, 3, 2):
                send(ref, ref, *sems[1], beside(axis, d))
        total = att_ref.at[0 : 2 if chunk < CHUNKS - 1 else 3, :, :, whole]
        drains.append((total, sems[1][0]))
        yield
        wait_bytes(total, sems[1][1])
        if chunk == CHUNKS - 1:
            return
        for lane, axis in enumerate("yx"):
            for d, share in ((1, pl.ds(0, 2)), (3, pl.ds(2, 2))):
                ref = lines[lane]((getattr(me, axis) + 4 - d) % 4, share)
                send(ref, ref, *sems[2], beside(axis, d))
        total = att_ref.at[0:1, :, :, whole]
        drains.append((total, sems[2][0]))
        yield
        wait_bytes(total, sems[2][1])

    def partial_out(chunk, half):
        where = pl.ds(chunk * CHUNK, CHUNK)
        return dot_last(att_ref[:, :, :, where].reshape(512, CHUNK), weight_ref[half, :, where])

    active = []
    for chunk in range(CHUNKS):
        rows = pl.ds(chunk * ROWS, ROWS)
        attend([(rows, quarter(3)), (rows, quarter(2))])
        for other in active[-2:]:
            next(other)
        if chunk == 0:
            value_copy.wait()
        attended_values(chunk, acc_ref, sum_ref, value_ref, att_ref, (me.x, me.y))
        active.append(exchange(chunk))
        next(active[-1])
    weight_copy.wait()
    next(active[2])
    next(active[3])
    for chunk in range(CHUNKS - 1):
        for _ in active[chunk]:
            pass
        if chunk == 0:
            wait_bytes(weight_ref.at[zh], weight_sem.at[1])

        @pl.loop(0, 2)
        def _(half):
            term = partial_out(chunk, half)
            total_ref[half] = term if chunk == 0 else total_ref[half] + term
    for _ in active[-1]:
        pass
    for far in (1, 0):
        half = 1 - zh if far else zh
        total_ref[half] = total_ref[half] + partial_out(CHUNKS - 1, half)
        for flip_z in (1, 0):
            for flip_c in (1, 0):
                target_l = 1 - zl if flip_z else zl
                target_c = 1 - me.c if flip_c else me.c
                slot = 4 * far + 2 * flip_z + flip_c
                if slot == 0:
                    continue
                rows = pl.ds(pl.multiple_of((target_l * 2 + target_c) * 128, 128), 128)
                part_ref[slot] = total_ref[half, rows, :].astype(BF)
                send(
                    part_ref.at[slot], land_ref.at[slot], rs_sem.at[0], rs_sem.at[1],
                    me.at(z=half * 2 + target_l, c=target_c),
                )
    wait_bytes(land_ref.at[1:8], rs_sem.at[1])
    drains.append((land_ref.at[1:8], rs_sem.at[0]))
    own_rows = pl.ds(pl.multiple_of((zl * 2 + me.c) * 128, 128), 128)
    for far in (0, 1):
        result = land_ref[4 * far + 1].astype(F32) + land_ref[4 * far + 2].astype(F32)
        result = result + land_ref[4 * far + 3].astype(F32)
        result = result + (land_ref[4].astype(F32) if far else total_ref[zh, own_rows, :])
        out_ref[:, 1 - zh if far else zh] = result.astype(BF).reshape(4, 32, 224)
    for ref, sem in drains:
        wait_bytes(ref, sem)


SCALE = 192**-0.5 * 1.4426950408889634
LAST = (((1,), (1,)), ((), ()))


def dot(a, b):
    return jnp.dot(a, b, preferred_element_type=jnp.float32)


def dot_last(a, b):
    return lax.dot_general(a, b, LAST, preferred_element_type=jnp.float32)


def latent_queries(low, high, q_ref, key_ref, qlat_ref):
    @pl.loop(low, high, unroll=4)
    def _(h):
        rows = pl.ds(pl.multiple_of(h * 32, 32), 32)
        qlat_ref[rows, :] = dot(q_ref[rows, 0:128], key_ref[h]).astype(BF)


def new_keys(q_ref, new_ref, qlat_ref, acc_ref, max_ref, sum_ref):
    @pl.loop(0, CHUNKS)
    def _(r):
        rows = pl.ds(pl.multiple_of(r * ROWS, ROWS), ROWS)
        scores = dot_last(qlat_ref[rows, :], new_ref[:, 0:512])
        scores = (scores + dot_last(q_ref[rows, 128:192], new_ref[:, 512:576])) * SCALE
        row = lax.broadcasted_iota(jnp.int32, (ROWS, 32), 0) % 32
        key = lax.broadcasted_iota(jnp.int32, (ROWS, 32), 1)
        visible = (row // 4 == key // 4) & (key <= row)
        top = jnp.max(jnp.where(visible, scores, -jnp.inf), axis=1, keepdims=True)
        e = jnp.where(visible, jnp.exp2(jnp.where(visible, scores, top) - top), 0.0)
        max_ref[rows, :] = jnp.broadcast_to(top, (ROWS, 128))
        sum_ref[rows, :] = jnp.broadcast_to(jnp.sum(e, axis=1, keepdims=True), (ROWS, 128))
        acc_ref[rows, :] = dot(e.astype(BF), new_ref[:, 0:512])


def attend_rows(q_ref, qlat_ref, lat_ref, rot_ref, acc_ref, max_ref, sum_ref, items):
    scores = [
        [dot_last(qlat_ref[rows, :], lat_ref[keys, :]) + dot(q_ref[rows, 128:192], rot_ref[:, keys]) for keys in key_slices]
        for rows, key_slices in items
    ]
    for (rows, key_slices), parts in zip(items, scores):
        old = max_ref[rows, :]
        top = functools.reduce(jnp.maximum, [jnp.max(s, axis=1, keepdims=True) for s in parts])
        new = jnp.maximum(old, top * SCALE)
        max_ref[rows, :] = new
        shrink = jnp.exp2(old - new)
        total = sum_ref[rows, :] * shrink
        acc = acc_ref[rows, :] * shrink[:, 0:1]
        for s, keys in zip(parts, key_slices):
            e = jnp.exp2(s * SCALE - new[:, 0:1])
            total = total + jnp.sum(e, axis=1, keepdims=True)
            acc = acc + dot(e.astype(BF), lat_ref[keys, :])
        sum_ref[rows, :] = total
        acc_ref[rows, :] = acc


def attended_values(chunk, acc_ref, sum_ref, value_ref, att_ref, place):
    heads = 32 // CHUNKS

    @pl.loop(chunk * heads, (chunk + 1) * heads, unroll=4)
    def _(h):
        rows = pl.ds(pl.multiple_of(h * 32, 32), 32)
        context = (acc_ref[rows, :] / sum_ref[rows, 0:1]).astype(BF)
        cols = pl.ds(pl.multiple_of(h * 128, 128), 128)
        att_ref[place + (slice(None), cols)] = dot(context, value_ref[h]).astype(BF)


def layer(owner_index, queries, new_kv, key_up, value_up, out_weight, latent, rope):
    sem = pltpu.SemaphoreType.DMA
    vm = pltpu.VMEM
    scratch = [
        vm((1024, 192), BF),
        vm((32, 576), BF),
        vm((32, 32, 192), F32),
        vm((8192, 512), BF),
        vm((64, 8192), BF),
        vm((32, 128, 512), BF),
        vm((32, 512, 128), BF),
        vm((2, 224, 4096), BF),
        vm((1024, 512), BF),
        vm((1024, 512), F32),
        vm((1024, 128), F32),
        vm((1024, 128), F32),
        vm((4, 4, 32, 4096), BF),
        vm((2, 512, 224), F32),
        vm((8, 128, 224), BF),
        vm((8, 128, 224), BF),
        sem((3,)),
        sem((2,)),
        sem((12,)),
        sem((12,)),
        sem((12,)),
        sem((12,)),
        sem((12,)),
        sem((3,)),
        sem((3,)),
        sem((5,)),
        sem((5,)),
        sem((3 * CHUNKS,)),
        sem((3 * CHUNKS,)),
        sem((2,)),
    ]
    for slots, held in landing_shapes():
        scratch += [vm(slots, BF), vm(held, BF)]
    hbm = pl.BlockSpec(memory_space=pl.ANY)
    vmem = pl.BlockSpec(memory_space=pltpu.VMEM)
    return pl.pallas_call(
        layer_kernel,
        out_shape=jax.ShapeDtypeStruct((4, 2, 32, 224), BF),
        in_specs=[pl.BlockSpec(memory_space=pltpu.SMEM), vmem, vmem] + [hbm] * 5,
        out_specs=vmem,
        scratch_shapes=scratch,
        compiler_params=pltpu.CompilerParams(
            collective_id=0, has_side_effects=True, vmem_limit_bytes=60 << 20
        ),
        name="layer",
    )(owner_index, queries, new_kv, key_up, value_up, out_weight, latent, rope)


def body(queries, new_kv, owner_index, prefix_latent, prefix_rope, key_up, value_up, out_weight):
    samples, steps, heads, width = queries.shape
    out = layer(
        owner_index, queries.reshape(samples * steps, heads, width), new_kv, key_up, value_up, out_weight.T,
        prefix_latent[0], prefix_rope[0],
    )
    return out.reshape(64, steps, -1)


def solution(mesh):
    return jax.shard_map(
        body,
        mesh=mesh,
        in_specs=(
            P("grp", None, "tp", None),
            P("grp", None, None),
            P(),
            P("grp", None, None),
            P("grp", None, None),
            P("tp", None, None),
            P("tp", None, None),
            P("tp", "grp"),
        ),
        out_specs=P("tp", None, "grp"),
        check_vma=False,
    )
```

```python
import functools
import jax
import jax.numpy as jnp
from jax import lax
from jax.experimental import pallas as pl
from jax.experimental.pallas import tpu as pltpu
from jax.sharding import PartitionSpec as P

MESH = pl.DeviceIdType.MESH
BF = jnp.bfloat16
F32 = jnp.float32
CHUNKS = 4
CHUNK = 4096 // CHUNKS
ROWS = 1024 // CHUNKS


class Coord:
    def __init__(self):
        g, t = lax.axis_index("grp"), lax.axis_index("tp")
        self.x, self.y, self.z, self.c = g // 8, (g // 2) % 4, (g % 2) * 2 + t // 2, t % 2

    def at(self, **moved):
        x, y, z, c = (moved.get(k, getattr(self, k)) for k in "xyzc")
        return (x * 8 + y * 2 + z // 2, (z % 2) * 2 + c)


ORDERS = (("x", "y", "z"), ("y", "z", "x"), ("z", "x", "y"), ("z", "x", "y"))
BASES = (0, 3072, 6144)
SHARE = ((768, 192, 96), (768, 384, 96), (512, 128, 32), (2048, 128))
ROPE = 3


def landing_shapes():
    shapes = []
    for region in range(4):
        for step in range(2 if region == ROPE else 3):
            share = SHARE[region][step]
            one = (32, share) if region == ROPE else (share, 256 if region == 2 else 128)
            slots = 16 if (region, step) == (ROPE, 1) else 2 if ORDERS[region][step] == "z" else 4
            shapes.append(((slots,) + one, one))
    return shapes


def wait_bytes(ref, sem):
    pltpu.make_async_copy(ref, ref, sem).wait()


def layer_kernel(
    owner_ref, query_ref, fresh_ref, key_hbm, value_hbm, weight_hbm, latent_hbm, rope_hbm, out_ref,
    q_ref, new_ref, wide_ref, lat_ref, rot_ref, key_ref, value_ref, weight_ref, qlat_ref, acc_ref, max_ref, sum_ref,
    att_ref, total_ref, part_ref, land_ref, local_sem, weight_sem, sc_send, sc_recv, sc_own,
    ag_send, ag_recv, last_send, last_recv, sw_send, sw_recv, ex_send, ex_recv, rs_sem, *landings
):
    me = Coord()
    zh, zl = me.z // 2, me.z % 2
    owner = owner_ref[0]
    owner_digit = {"x": owner // 8, "y": (owner // 2) % 4, "z": owner % 2}
    key_copy = pltpu.make_async_copy(key_hbm, key_ref, local_sem.at[0])
    value_copy = pltpu.make_async_copy(value_hbm, value_ref, local_sem.at[1])
    weight_copy = pltpu.make_async_copy(weight_hbm, weight_ref.at[zh], local_sem.at[2])
    drains = []

    def send(src, dst, send_sem, recv_sem, device):
        copy = pltpu.make_async_remote_copy(
            src_ref=src, dst_ref=dst, send_sem=send_sem, recv_sem=recv_sem, device_id=device, device_id_type=MESH
        )
        copy.start()
        return copy

    def beside(axis, d):
        return me.at(**{axis: (getattr(me, axis) + d) % 4})

    barrier = pltpu.get_barrier_semaphore()
    peers = [beside(a, d) for a in "xyz" for d in (1, 2, 3)]
    peers += [me.at(z=(me.z + d) % 4, c=1 - me.c) for d in range(4)]
    peers += [me.at(x=(me.x + i) % 4, y=(me.y + j) % 4) for i in (1, 2, 3) for j in (1, 2, 3)]
    for peer in peers:
        pl.semaphore_signal(barrier, inc=1, device_id=peer, device_id_type=MESH)
    pl.semaphore_wait(barrier, len(peers))

    cols = pl.ds(pl.multiple_of(256 * me.c, 256), 256)
    rope_rows = pl.ds(pl.multiple_of(32 * me.c, 32), 32)

    def own_digit(axis):
        return zh if axis == "z" else getattr(me, axis)

    tile = pl.ds(pl.multiple_of(256 * me.c + 128 * zl, 128), 128)

    def source(region, digit):
        if region == ROPE:
            return rope_hbm.at[rope_rows, pl.ds(pl.multiple_of(4096 * digit + 2048 * zl, 128), 2048)]
        if region == 2:
            return latent_hbm.at[pl.ds(pl.multiple_of(6144 + 1024 * digit + 512 * zl, 512), 512), cols]
        return latent_hbm.at[pl.ds(pl.multiple_of(BASES[region] + 768 * digit, 256), 768), tile]

    def part(region, step, digit):
        if step == 0:
            return source(region, digit)
        held = landings[2 * (region * 3 + step - 1) + 1]
        share = SHARE[region][step]
        if region == ROPE:
            return held.at[:, pl.ds(pl.multiple_of(digit * share, 128), share)]
        return held.at[pl.ds(pl.multiple_of(digit * share, 32), share)]

    def scatter(region, step):
        axis = ORDERS[region][step]
        index = region * 3 + step
        slots = landings[2 * index]
        mine = own_digit(axis)
        if axis == "z":
            send(part(region, step, 1 - zh), slots.at[mine], sc_send.at[index], sc_recv.at[index], beside("z", 2))
        else:
            for d in (1, 3, 2):
                digit = (mine + d) % 4
                send(part(region, step, digit), slots.at[mine], sc_send.at[index], sc_recv.at[index], beside(axis, d))
        pltpu.make_async_copy(part(region, step, mine), slots.at[mine], sc_own.at[index]).start()
        others = slots.at[pl.ds(0, slots.shape[0] - 1)]
        drains.append((others, sc_send.at[index]))

    def pick(region, step):
        index = region * 3 + step
        slots = landings[2 * index]
        wait_bytes(slots.at[0], sc_own.at[index])
        wait_bytes(slots.at[pl.ds(0, slots.shape[0] - 1)], sc_recv.at[index])
        return slots[owner_digit[ORDERS[region][step]]]

    def extent(region, level):
        if region in (0, 1):
            return (768, (192, 384)[region], 96)[level - 1], level == 3 or (region, level) == (1, 2)
        return (32, 128)[region - 2] * 4 ** (3 - level), False

    def block(region, level, digits):
        count, narrow = extent(region, level)
        if region == ROPE or region == 2:
            place = digits[0] * 16
            for i in range(1, level):
                place = place + digits[i] * 4 ** (2 - i)
            if region == ROPE:
                return rot_ref.at[rope_rows, pl.ds(pl.multiple_of(128 * place, 128), count)]
            return lat_ref.at[pl.ds(pl.multiple_of(6144 + 32 * place, 32), count), cols]
        start = BASES[region] + digits[0] * 768
        if region == 0:
            start = start + (digits[1] * 192 if level > 1 else 0) + (zh * 96 if level > 2 else 0)
        else:
            start = start + (zh * 384 if level > 1 else 0) + (digits[2] * 96 if level > 2 else 0)
        return lat_ref.at[pl.ds(pl.multiple_of(start, 32), count), tile if narrow else cols]

    digits = [tuple(getattr(me, a) for a in o) for o in ORDERS]

    def three(region, level):
        count, narrow = extent(region, level)
        if region == ROPE:
            return rot_ref.at[0:32, 0 : 3 * count]
        return lat_ref.at[0 : 3 * count, 0 : 128 if narrow else 256]

    def gather(region, level):
        ref = block(region, level, digits[region])
        sems = ag_send.at[region * 3 + level - 1], ag_recv.at[region * 3 + level - 1]
        for d in (1, 3, 2):
            send(ref, ref, *sems, beside(ORDERS[region][level - 1], d))
        drains.append((three(region, level), sems[0]))

    def gathered(region, level):
        wait_bytes(three(region, level), ag_recv.at[region * 3 + level - 1])

    plane = [(i, j) for i in range(4) for j in range(4) if i or j]

    def rope_scatter():
        held, slots = landings[2 * 9 + 1], landings[2 * 10]
        mine = me.x * 4 + me.y
        for i, j in plane:
            x, y = (me.x + i) % 4, (me.y + j) % 4
            lanes = pl.ds(pl.multiple_of(128 * (x * 4 + y), 128), 128)
            send(held.at[:, lanes], slots.at[mine], sc_send.at[10], sc_recv.at[10], me.at(x=x, y=y))
        lanes = pl.ds(pl.multiple_of(128 * mine, 128), 128)
        pltpu.make_async_copy(held.at[:, lanes], slots.at[mine], sc_own.at[10]).start()
        drains.append((slots.at[0:15], sc_send.at[10]))

    def rope_pick():
        slots = landings[2 * 10]
        wait_bytes(slots.at[0], sc_own.at[10])
        wait_bytes(slots.at[0:15], sc_recv.at[10])
        return slots[owner_digit["x"] * 4 + owner_digit["y"]]

    def rope_plane():
        ref = block(ROPE, 3, digits[ROPE])
        sems = ag_send.at[ROPE * 3 + 2], ag_recv.at[ROPE * 3 + 2]
        for i, j in plane:
            send(ref, ref, *sems, me.at(x=(me.x + i) % 4, y=(me.y + j) % 4))
        drains.append((rot_ref.at[0:32, 0:1920], sems[0]))

    def swap(d):
        for region in range(3):
            ref = block(region, 1, ((digits[region][0] + 4 - d) % 4, 0, 0))
            send(ref, ref, sw_send.at[d], sw_recv.at[d], me.at(c=1 - me.c))
        drains.append((lat_ref.at[0:2048, 0:256], sw_send.at[d]))

    def swapped(d):
        wait_bytes(lat_ref.at[0:2048, 0:256], sw_recv.at[d])

    def send_weight(low, high):
        where = pl.ds(16 * low, 16 * (high - low))
        send(weight_hbm.at[where], weight_ref.at[zh, where], weight_sem.at[0], weight_sem.at[1], beside("z", 2))

    def last(region, distances):
        ref = block(region, 1, digits[region])
        for d in distances:
            send(ref, ref, last_send.at[d - 1], last_recv.at[d - 1], beside(ORDERS[region][0], d))

    for region in range(4):
        scatter(region, 0)
    key_copy.start()
    value_copy.start()
    weight_copy.start()
    wide_ref[...] = query_ref[...].astype(F32)

    @pl.loop(0, 32, unroll=4)
    def _(h):
        q_ref[pl.ds(pl.multiple_of(h * 32, 32), 32), :] = wide_ref[:, h, :].astype(BF)

    for sample in range(8):
        wide_ref[0, 4 * sample : 4 * sample + 4, :] = fresh_ref[sample, :, 0:192].astype(F32)
        wide_ref[1, 4 * sample : 4 * sample + 4, :] = fresh_ref[sample, :, 192:384].astype(F32)
        wide_ref[2, 4 * sample : 4 * sample + 4, :] = fresh_ref[sample, :, 384:576].astype(F32)
    for third in range(3):
        new_ref[:, 192 * third : 192 * third + 192] = wide_ref[third].astype(BF)
    key_copy.wait()
    latent_queries(0, 16, q_ref, key_ref, qlat_ref)
    landings[2 * 9 + 1][...] = pick(ROPE, 0)
    rope_scatter()
    for region in range(3):
        landings[2 * (region * 3) + 1][...] = pick(region, 0)
        scatter(region, 1)
    send_weight(0, 1)
    latent_queries(16, 32, q_ref, key_ref, qlat_ref)
    home = block(ROPE, 3, digits[ROPE])
    home[...] = rope_pick()
    rope_plane()
    for region in range(3):
        landings[2 * (region * 3 + 1) + 1][...] = pick(region, 1)
        scatter(region, 2)
    send_weight(1, 2)
    wait_bytes(rot_ref.at[0:32, 0:1920], ag_recv.at[ROPE * 3 + 2])
    for region in range(3):
        home = block(region, 3, digits[region])
        home[...] = pick(region, 2)
        gather(region, 3)
    gather(ROPE, 1)
    new_keys(q_ref, new_ref, qlat_ref, acc_ref, max_ref, sum_ref)
    for region in range(3):
        gathered(region, 3)
        gather(region, 2)
    gathered(ROPE, 1)
    send(rot_ref.at[rope_rows], rot_ref.at[rope_rows], sw_send.at[4], sw_recv.at[4], me.at(c=1 - me.c))
    drains.append((rot_ref.at[0:32], sw_send.at[4]))
    send_weight(2, 3)
    for region in range(3):
        gathered(region, 2)
        last(region, (1, 3))
    for d in (1, 2, 3):
        drains.append((lat_ref.at[0:2048, 0:256], last_send.at[d - 1]))
    swap(0)

    def arrived(d):
        wait_bytes(lat_ref.at[0:2048, 0:256], last_recv.at[d - 1])

    def quarter(d):
        sizes = (768, 768, 512)
        starts = [BASES[r] + sizes[r] * ((digits[r][0] + 4 - d) % 4) for r in range(3)]
        return [pl.ds(pl.multiple_of(s, 256), n) for s, n in zip(starts, sizes)]

    attend = functools.partial(
        attend_rows, q_ref, qlat_ref, lat_ref, rot_ref, acc_ref, max_ref, sum_ref
    )
    def rows_of(i):
        return pl.ds(pl.multiple_of(i * 256, 256), 256)

    wait_bytes(rot_ref.at[0:32], sw_recv.at[4])
    swapped(0)

    def half(i, d):
        attend([(rows_of(2 * i), quarter(d)), (rows_of(2 * i + 1), quarter(d))])

    half(0, 0)
    for region in range(3):
        last(region, (2,))
    half(1, 0)
    arrived(1)
    swap(1)
    arrived(3)
    swap(3)
    swapped(1)
    half(0, 1)
    arrived(2)
    swap(2)
    send_weight(3, 5)
    attend([(rows_of(2), quarter(1))])
    swapped(3)
    swapped(2)
    send_weight(5, 14)
    drains.append((weight_ref.at[zh], weight_sem.at[0]))

    def exchange(chunk):
        cols = [pl.ds(chunk * CHUNK + lane * (CHUNK // 2), CHUNK // 2) for lane in (0, 1)]
        whole = pl.ds(chunk * CHUNK, CHUNK)
        sems = [(ex_send.at[chunk * 3 + i], ex_recv.at[chunk * 3 + i]) for i in range(3)]
        for lane, axis in enumerate("xy"):
            ref = att_ref.at[me.x, me.y, :, cols[lane]]
            for d in (1, 3, 2):
                send(ref, ref, *sems[0], beside(axis, d))
        total = att_ref.at[0, 0:3, :, whole]
        drains.append((total, sems[0][0]))
        yield
        wait_bytes(total, sems[0][1])
        lines = [lambda y, s=slice(None): att_ref.at[s, y, :, cols[0]], lambda x, s=slice(None): att_ref.at[x, s, :, cols[1]]]
        for lane, axis in enumerate("yx"):
            ref = lines[lane](getattr(me, axis))
            for d in (1, 3) if chunk < CHUNKS - 1 else (1, 3, 2):
                send(ref, ref, *sems[1], beside(axis, d))
        total = att_ref.at[0 : 2 if chunk < CHUNKS - 1 else 3, :, :, whole]
        drains.append((total, sems[1][0]))
        yield
        wait_bytes(total, sems[1][1])
        if chunk == CHUNKS - 1:
            return
        for lane, axis in enumerate("yx"):
            for d, share in ((1, pl.ds(0, 2)), (3, pl.ds(2, 2))):
                ref = lines[lane]((getattr(me, axis) + 4 - d) % 4, share)
                send(ref, ref, *sems[2], beside(axis, d))
        total = att_ref.at[0:1, :, :, whole]
        drains.append((total, sems[2][0]))
        yield
        wait_bytes(total, sems[2][1])

    def partial_out(chunk, half):
        where = pl.ds(chunk * CHUNK, CHUNK)
        return dot_last(att_ref[:, :, :, where].reshape(512, CHUNK), weight_ref[half, :, where])

    active = []
    for chunk in range(CHUNKS):
        rows = pl.ds(chunk * ROWS, ROWS)
        if chunk == CHUNKS - 1:
            attend([(rows, quarter(1)), (rows, quarter(3))])
            attend([(rows, quarter(2))])
        else:
            attend([(rows, quarter(3)), (rows, quarter(2))])
        for other in active[-2:]:
            next(other)
        if chunk == 0:
            value_copy.wait()
        attended_values(chunk, acc_ref, sum_ref, value_ref, att_ref, (me.x, me.y))
        active.append(exchange(chunk))
        next(active[-1])
    weight_copy.wait()
    next(active[2])
    next(active[3])
    for chunk in range(CHUNKS - 1):
        for _ in active[chunk]:
            pass
        if chunk == 0:
            wait_bytes(weight_ref.at[zh], weight_sem.at[1])

        @pl.loop(0, 2)
        def _(half):
            term = partial_out(chunk, half)
            total_ref[half] = term if chunk == 0 else total_ref[half] + term
    for _ in active[-1]:
        pass
    for far in (1, 0):
        half = 1 - zh if far else zh
        total_ref[half] = total_ref[half] + partial_out(CHUNKS - 1, half)
        for flip_z in (1, 0):
            for flip_c in (1, 0):
                target_l = 1 - zl if flip_z else zl
                target_c = 1 - me.c if flip_c else me.c
                slot = 4 * far + 2 * flip_z + flip_c
                if slot == 0:
                    continue
                rows = pl.ds(pl.multiple_of((target_l * 2 + target_c) * 128, 128), 128)
                part_ref[slot] = total_ref[half, rows, :].astype(BF)
                send(
                    part_ref.at[slot], land_ref.at[slot], rs_sem.at[0], rs_sem.at[1],
                    me.at(z=half * 2 + target_l, c=target_c),
                )
    wait_bytes(land_ref.at[1:8], rs_sem.at[1])
    drains.append((land_ref.at[1:8], rs_sem.at[0]))
    own_rows = pl.ds(pl.multiple_of((zl * 2 + me.c) * 128, 128), 128)
    for far in (0, 1):
        result = land_ref[4 * far + 1].astype(F32) + land_ref[4 * far + 2].astype(F32)
        result = result + land_ref[4 * far + 3].astype(F32)
        result = result + (land_ref[4].astype(F32) if far else total_ref[zh, own_rows, :])
        out_ref[:, 1 - zh if far else zh] = result.astype(BF).reshape(4, 32, 224)
    for ref, sem in drains:
        wait_bytes(ref, sem)


SCALE = 192**-0.5 * 1.4426950408889634
LAST = (((1,), (1,)), ((), ()))


def dot(a, b):
    return jnp.dot(a, b, preferred_element_type=jnp.float32)


def dot_last(a, b):
    return lax.dot_general(a, b, LAST, preferred_element_type=jnp.float32)


def latent_queries(low, high, q_ref, key_ref, qlat_ref):
    @pl.loop(low, high, unroll=4)
    def _(h):
        rows = pl.ds(pl.multiple_of(h * 32, 32), 32)
        qlat_ref[rows, :] = dot(q_ref[rows, 0:128], key_ref[h]).astype(BF)


def new_keys(q_ref, new_ref, qlat_ref, acc_ref, max_ref, sum_ref):
    @pl.loop(0, CHUNKS)
    def _(r):
        rows = pl.ds(pl.multiple_of(r * ROWS, ROWS), ROWS)
        scores = dot_last(qlat_ref[rows, :], new_ref[:, 0:512])
        scores = (scores + dot_last(q_ref[rows, 128:192], new_ref[:, 512:576])) * SCALE
        row = lax.broadcasted_iota(jnp.int32, (ROWS, 32), 0) % 32
        key = lax.broadcasted_iota(jnp.int32, (ROWS, 32), 1)
        visible = (row // 4 == key // 4) & (key <= row)
        top = jnp.max(jnp.where(visible, scores, -jnp.inf), axis=1, keepdims=True)
        e = jnp.where(visible, jnp.exp2(jnp.where(visible, scores, top) - top), 0.0)
        max_ref[rows, :] = jnp.broadcast_to(top, (ROWS, 128))
        sum_ref[rows, :] = jnp.broadcast_to(jnp.sum(e, axis=1, keepdims=True), (ROWS, 128))
        acc_ref[rows, :] = dot(e.astype(BF), new_ref[:, 0:512])


def attend_rows(q_ref, qlat_ref, lat_ref, rot_ref, acc_ref, max_ref, sum_ref, items):
    scores = [
        [dot_last(qlat_ref[rows, :], lat_ref[keys, :]) + dot(q_ref[rows, 128:192], rot_ref[:, keys]) for keys in key_slices]
        for rows, key_slices in items
    ]
    for (rows, key_slices), parts in zip(items, scores):
        old = max_ref[rows, :]
        top = functools.reduce(jnp.maximum, [jnp.max(s, axis=1, keepdims=True) for s in parts])
        new = jnp.maximum(old, top * SCALE)
        max_ref[rows, :] = new
        shrink = jnp.exp2(old - new)
        total = sum_ref[rows, :] * shrink
        acc = acc_ref[rows, :] * shrink[:, 0:1]
        for s, keys in zip(parts, key_slices):
            e = jnp.exp2(s * SCALE - new[:, 0:1])
            total = total + jnp.sum(e, axis=1, keepdims=True)
            acc = acc + dot(e.astype(BF), lat_ref[keys, :])
        sum_ref[rows, :] = total
        acc_ref[rows, :] = acc


def attended_values(chunk, acc_ref, sum_ref, value_ref, att_ref, place):
    heads = 32 // CHUNKS

    @pl.loop(chunk * heads, (chunk + 1) * heads, unroll=4)
    def _(h):
        rows = pl.ds(pl.multiple_of(h * 32, 32), 32)
        context = (acc_ref[rows, :] / sum_ref[rows, 0:1]).astype(BF)
        cols = pl.ds(pl.multiple_of(h * 128, 128), 128)
        att_ref[place + (slice(None), cols)] = dot(context, value_ref[h]).astype(BF)


def layer(owner_index, queries, new_kv, key_up, value_up, out_weight, latent, rope):
    sem = pltpu.SemaphoreType.DMA
    vm = pltpu.VMEM
    scratch = [
        vm((1024, 192), BF),
        vm((32, 576), BF),
        vm((32, 32, 192), F32),
        vm((8192, 512), BF),
        vm((64, 8192), BF),
        vm((32, 128, 512), BF),
        vm((32, 512, 128), BF),
        vm((2, 224, 4096), BF),
        vm((1024, 512), BF),
        vm((1024, 512), F32),
        vm((1024, 128), F32),
        vm((1024, 128), F32),
        vm((4, 4, 32, 4096), BF),
        vm((2, 512, 224), F32),
        vm((8, 128, 224), BF),
        vm((8, 128, 224), BF),
        sem((3,)),
        sem((2,)),
        sem((12,)),
        sem((12,)),
        sem((12,)),
        sem((12,)),
        sem((12,)),
        sem((3,)),
        sem((3,)),
        sem((5,)),
        sem((5,)),
        sem((3 * CHUNKS,)),
        sem((3 * CHUNKS,)),
        sem((2,)),
    ]
    for slots, held in landing_shapes():
        scratch += [vm(slots, BF), vm(held, BF)]
    hbm = pl.BlockSpec(memory_space=pl.ANY)
    vmem = pl.BlockSpec(memory_space=pltpu.VMEM)
    return pl.pallas_call(
        layer_kernel,
        out_shape=jax.ShapeDtypeStruct((4, 2, 32, 224), BF),
        in_specs=[pl.BlockSpec(memory_space=pltpu.SMEM), vmem, vmem] + [hbm] * 5,
        out_specs=vmem,
        scratch_shapes=scratch,
        compiler_params=pltpu.CompilerParams(
            collective_id=0, has_side_effects=True, vmem_limit_bytes=60 << 20
        ),
        name="layer",
    )(owner_index, queries, new_kv, key_up, value_up, out_weight, latent, rope)


def body(queries, new_kv, owner_index, prefix_latent, prefix_rope, key_up, value_up, out_weight):
    samples, steps, heads, width = queries.shape
    out = layer(
        owner_index, queries.reshape(samples * steps, heads, width), new_kv, key_up, value_up, out_weight.T,
        prefix_latent[0], prefix_rope[0],
    )
    return out.reshape(64, steps, -1)


def solution(mesh):
    return jax.shard_map(
        body,
        mesh=mesh,
        in_specs=(
            P("grp", None, "tp", None),
            P("grp", None, None),
            P(),
            P("grp", None, None),
            P("grp", None, None),
            P("tp", None, None),
            P("tp", None, None),
            P("tp", "grp"),
        ),
        out_specs=P("tp", None, "grp"),
        check_vma=False,
    )
```
